256 devices in a mesh: src: 8 (over x, y_hi), snk: 8 (over z), mom: 4 (over y_lo, core).
Axes of the slice: x: 4, y: 4 (y_hi: 2, y_lo: 2; y = y_hi * 2 + y_lo), z: 8, core: 2. Of those that a mesh axis runs over, the one named last changes fastest.
Arguments:
- peram_blocks: bfloat16 [32, 8, 2, 512, 512], P('src', 'snk'), may hold values from -5 to 5
- projections: bfloat16 [32, 4, 4, 2, 128, 128], P('src', 'mom'), may hold values from -0.5 to 0.5
- gamma_index: int32 [4, 4], replicated, may hold values from 0 to 15
- partner: int32 [4], P('mom'), may hold values from 0 to 3, each once
- separations: int32 [4], replicated, may hold values from 1 to 31, as said below
Outputs:
- correlator: float32 [32, 4, 4, 2], P(None, None, 'mom')
The draws below stay inside these ranges and needn't reach their ends.
Inputs may be any that keep to these rules, and one draw needn't show every extreme that they name: Each operator appears once as the partner of a source operator. separations count source time slices; sink slices are taken modulo 32.
All inputs are finite; a program needn't handle non-finite values.
Results may differ from the reference program's by a relative error of at most 0.007.
Values may be sent and summed in bfloat16 or wider, within the bound.
A program may use at most 64 MiB of HBM per device.

```python
import jax
import jax.numpy as jnp
import numpy as np
from jax import lax

NEV = 128
NTERM = 4
NSEP = 4
M = 512
NT = 32
NOFF = 8
NMOM = 4


def draw_separations(key, part):
    key = jax.random.fold_in(key, 7)
    extremes = jnp.array([NT - 1, 1], dtype=jnp.int32)
    middle = jax.random.randint(key, (NSEP,), 1, NT, dtype=jnp.int32)
    values = jnp.concatenate([extremes, middle[2:]])
    shuffled = jax.random.permutation(jax.random.fold_in(key, 1), NSEP)
    return values[shuffled].astype(jnp.int32)


def plant(values, own_key, smallest, top_value):
    dims = values.shape
    index_at = [jax.random.randint(jax.random.fold_in(own_key, axis), (), 0, dims[axis]) for axis in range(len(dims))]
    values = values.at[tuple(index_at)].set(smallest)
    longest = dims.index(max(dims))
    index_at[longest] = (index_at[longest] + 1) % dims[longest]
    return values.at[tuple(index_at)].set(top_value)


def level_of(rng, extent, cuts, least, high):
    level = 1.0
    for dim, parts in cuts:
        draws = jax.random.uniform(jax.random.fold_in(jax.random.fold_in(rng, 6), dim), (parts,), jnp.float32, least / len(cuts), high / len(cuts))
        level = level * jnp.repeat(jnp.exp(draws), extent[dim] // parts).reshape((-1,) + (1,) * (len(extent) - 1 - dim))
    return level


def centred(rng, dims, spread, bound, pieces=(), held_as=jnp.bfloat16):
    loudness = level_of(rng, dims, pieces, -0.22, 0.18) if pieces else 1.0
    values = jax.random.normal(rng, dims, jnp.float32) * spread * loudness
    return jnp.minimum(jnp.maximum(values, -bound), bound).astype(held_as)


def setup_inputs(seed: int = 0) -> dict:
    key_list = jax.random.split(jax.random.key(seed), 6)
    return {
        "peram_blocks": centred(key_list[0], (NT, NOFF, 2, M, M), 0.35, 5.0, ((0, 8), (1, 8))),
        "projections": centred(key_list[1], (NT, NMOM, NTERM, 2, NEV, NEV), NEV ** -0.5, 0.5, ((0, 8), (1, 4))),
        "gamma_index": plant(jax.random.randint(key_list[2], (NMOM, NTERM), 0, 16), jax.random.fold_in(key_list[2], 1), 0, 15).astype(jnp.int32),
        "partner": jax.random.permutation(key_list[3], NMOM).astype(jnp.int32),
        "separations": draw_separations(jax.random.fold_in(key_list[5], 71), 0),
    }


def dirac_table():
    zero_matrix = np.zeros((4, 4))
    unit_real = np.eye(4)
    gamma_one = (zero_matrix, np.array([[0, 0, 0, 1], [0, 0, 1, 0], [0, -1, 0, 0], [-1, 0, 0, 0]], dtype=np.float32))
    gamma_two = (np.array([[0, 0, 0, -1], [0, 0, 1, 0], [0, 1, 0, 0], [-1, 0, 0, 0]], dtype=np.float32), zero_matrix)
    gamma_three = (zero_matrix, np.array([[0, 0, 1, 0], [0, 0, 0, -1], [-1, 0, 0, 0], [0, 1, 0, 0]], dtype=np.float32))
    gamma_four = (np.array([[0, 0, 1, 0], [0, 0, 0, 1], [1, 0, 0, 0], [0, 1, 0, 0]], dtype=np.float32), zero_matrix)
    factors = (gamma_one, gamma_two, gamma_three, gamma_four)
    real_list = []
    imag_list = []
    for gamma_code in range(16):
        real_now = unit_real
        imag_now = zero_matrix
        for position in range(4):
            if (gamma_code >> position) & 1:
                factor_real, factor_imag = factors[position]
                next_real = real_now @ factor_real - imag_now @ factor_imag
                next_imag = real_now @ factor_imag + imag_now @ factor_real
                real_now = next_real
                imag_now = next_imag
        real_list.append(real_now)
        imag_list.append(imag_now)
    return np.stack([np.stack(real_list), np.stack(imag_list)], axis=1).astype(np.float32)


def build_elementals(projections, gamma_index):
    codes = jnp.arange(16, dtype=jnp.int32)
    one_hot = (gamma_index[:, :, None] == codes[None, None, :]).astype(jnp.float32)
    spin_part = jnp.einsum('prg,gcst->prcst', one_hot, jnp.asarray(dirac_table()).astype(jnp.float32))
    proj_real = projections[:, :, :, 0].astype(jnp.float32)
    proj_imag = projections[:, :, :, 1].astype(jnp.float32)
    form = 'prst,wpref->wpsetf'
    real_part = jnp.einsum(form, spin_part[:, :, 0], proj_real) - jnp.einsum(form, spin_part[:, :, 1], proj_imag)
    imag_part = jnp.einsum(form, spin_part[:, :, 0], proj_imag) + jnp.einsum(form, spin_part[:, :, 1], proj_real)
    full_width = 4 * projections.shape[-1]
    shape_out = (projections.shape[0], projections.shape[1], full_width, full_width)
    stacked = jnp.stack([real_part.reshape(shape_out), imag_part.reshape(shape_out)], axis=2)
    return stacked.astype(jnp.bfloat16)


def complex_product(block, elementals):
    block_wide = block.astype(jnp.float32)
    elem_wide = lax.optimization_barrier(elementals).astype(jnp.float32)
    form = 'xc,ocy->oxy'
    real_part = jnp.einsum(form, block_wide[0], elem_wide[:, 0]) - jnp.einsum(form, block_wide[1], elem_wide[:, 1])
    imag_part = jnp.einsum(form, block_wide[0], elem_wide[:, 1]) + jnp.einsum(form, block_wide[1], elem_wide[:, 0])
    return jnp.stack([real_part, imag_part], axis=1).astype(jnp.bfloat16)


def reference(peram_blocks, projections, gamma_index, partner, separations):
    def one_pair(flat_index):
        time_now = flat_index // NSEP
        sep_index = flat_index % NSEP
        time_back = (time_now + separations[sep_index]) % NT
        forward_block = peram_blocks[time_now, sep_index]
        backward_block = peram_blocks[time_back, NSEP + sep_index]
        elem_now = build_elementals(projections[time_now][None], gamma_index)[0]
        elem_back = build_elementals(projections[time_back][None], gamma_index)[0][partner]
        forward = lax.optimization_barrier(complex_product(forward_block, elem_now)).astype(jnp.float32)
        backward = lax.optimization_barrier(complex_product(backward_block, elem_back)).astype(jnp.float32)
        form = 'pxy,pyx->p'
        real_part = jnp.einsum(form, forward[:, 0], backward[:, 0]) - jnp.einsum(form, forward[:, 1], backward[:, 1])
        imag_part = jnp.einsum(form, forward[:, 0], backward[:, 1]) + jnp.einsum(form, forward[:, 1], backward[:, 0])
        return jnp.stack([real_part, imag_part], axis=-1) / M
    values = lax.map(one_pair, jnp.arange(NT * NSEP, dtype=jnp.int32))
    return values.reshape(NT, NSEP, NMOM, 2)
```

```python
import functools

import jax
import jax.numpy as jnp
import numpy as np
from jax import lax
from jax.experimental import pallas as pl
from jax.experimental.pallas import tpu as pltpu
from jax.sharding import PartitionSpec as P

MESH = pl.DeviceIdType.MESH
NSEP = 4
ROLE_B_PLANES = (6, 3, 0, 5)


def gamma_table():
    unit = np.eye(4, dtype=complex)
    one = np.array([[0, 0, 0, 1j], [0, 0, 1j, 0], [0, -1j, 0, 0], [-1j, 0, 0, 0]])
    two = np.array([[0, 0, 0, -1], [0, 0, 1, 0], [0, 1, 0, 0], [-1, 0, 0, 0]], dtype=complex)
    three = np.array([[0, 0, 1j, 0], [0, 0, 0, -1j], [-1j, 0, 0, 0], [0, 1j, 0, 0]])
    four = np.array([[0, 0, 1, 0], [0, 0, 0, 1], [1, 0, 0, 0], [0, 1, 0, 0]], dtype=complex)
    rows = []
    for code in range(16):
        value = unit
        for position, factor in enumerate((one, two, three, four)):
            if code >> position & 1:
                value = value @ factor
        pattern = int(np.flatnonzero(np.abs(value[:, 0]))[0])
        powers = [(1, 1j, -1, -1j).index(complex(value[s ^ pattern, s])) for s in range(4)]
        rows.append([pattern] + powers)
    return np.array(rows, dtype=np.int32).reshape(-1)


def body(
    sep_ref, gam_ref, part_ref, tab_ref, p_ref, e_ref, out_ref,
    e_in, p_in, e_snd, p_snd, pl_snd, el_snd, e1, p1, e2s, p2s, eloc, erem, prem, pn,
    fbuf, nbuf, ptr, partbuf, res, r1, t2, r2, lsem, ssem, rsem,
):
    src, z, mom = lax.axis_index("src"), lax.axis_index("snk"), lax.axis_index("mom")
    c, e = mom // 2, mom % 2
    u = 2 * src + c
    me = 4 * src + mom
    k = (z + 2) % 4
    sep = sep_ref[k]
    odd = sep & 1
    role_a = (z + z // 2 + z // 4) % 2
    is_a = role_a == 1
    shift = jnp.where(is_a, sep >> 1, 16 - ((sep + 1) >> 1))
    par_loc = jnp.where(is_a, 0, (1 + odd) & 1)
    par_rem = jnp.where(is_a, odd, 1)
    odd_own = sep_ref[z % 4] & 1
    snd_rem = jnp.where(z < NSEP, 1, odd_own)
    snd_loc = jnp.where(z < NSEP, 0, (1 + odd_own) & 1)
    z_even = 1 - z % 2
    z_rem = (z + 2 + 4 * z_even) % 8
    z_loc = (z + 6 + 4 * z_even) % 8

    def remote(src_ref, dst_ref, index, target):
        return pltpu.make_async_remote_copy(
            src_ref=src_ref, dst_ref=dst_ref, send_sem=ssem.at[index], recv_sem=rsem.at[index],
            device_id=target, device_id_type=MESH,
        )

    def arrived(ref, index):
        pltpu.make_async_copy(ref, ref, rsem.at[index]).wait()

    def left(ref, index):
        pltpu.make_async_copy(ref, ref, ssem.at[index]).wait()

    other_core = (src, z, 2 * c + 1 - e)
    other_chip = (src, z, 2 * (1 - c) + e)

    load_e = pltpu.make_async_copy(e_ref, e_in, lsem.at[0])
    load_e.start()
    load_p = pltpu.make_async_copy(
        p_ref.at[pl.ds(2 * c, 2), 0, :, pl.ds(pl.multiple_of(256 * e, 256), 256), :], p_in, lsem.at[1]
    )
    load_p.start()
    partbuf[mom] = jnp.full((8, 128), part_ref[0], jnp.int32)

    def send_partner(d, carry):
        remote(partbuf.at[mom], partbuf.at[mom], 0, (src, z, (mom + d) % 4)).start()
        return carry

    lax.fori_loop(1, 4, send_partner, 0)

    load_e.wait()
    for h in range(2):
        e_snd[h] = e_in[2 * h + par_rem]

    def send_e1(d, carry):
        i = (me + d) % 32
        rows = pl.ds(pl.multiple_of(32 * i, 32), 32)
        remote(e_snd.at[:, rows, :], e1.at[me], 1, (i // 4, z, i % 4)).start()
        return carry

    lax.fori_loop(1, 32, send_e1, 0)
    own_rows = pl.ds(pl.multiple_of(32 * me, 32), 32)
    e1[me] = e_snd[:, own_rows, :]

    load_p.wait()
    p_snd[...] = p_in[snd_rem]

    def send_p1(d, carry):
        j = (u + d) % 16
        rows = pl.ds(pl.multiple_of(16 * j, 16), 16)
        remote(p_snd.at[:, rows, :], p1.at[u], 2, (j // 2, z_rem, 2 * (j % 2) + e)).start()
        return carry

    lax.fori_loop(0, 16, send_p1, 0)

    eloc[mom] = e_in[2 * c + par_loc]
    el_snd[...] = e_in[2 * (1 - c) + par_loc]
    own_e = remote(eloc.at[mom], eloc.at[mom], 3, other_core)
    own_e.start()
    cross_e = remote(el_snd, eloc.at[mom], 4, other_chip)
    cross_e.start()
    half = pl.ds(pl.multiple_of(256 * e, 256), 256)
    other_half = pl.ds(pl.multiple_of(256 * (1 - e), 256), 256)
    for s in range(4):
        pl_snd[:, s] = p_in[snd_loc, :, :, pl.ds(128 * s, 128)]
    direct_p = remote(pl_snd, pn.at[pl.ds(0, 2), :, half, :], 5, (src, z_loc, mom))
    direct_p.start()

    arrived(partbuf.at[pl.ds(0, 3)], 0)
    partners = [partbuf[o, 0, 0] for o in range(4)]
    arrived(e1.at[pl.ds(0, 31)], 1)

    def rem_op(core, a):
        return jnp.where(is_a, jnp.where(core == 0, partners[2 * a], partners[2 * a + 1]), core + 2 * a)

    def pick_e(i, a):
        block = (i // 2 + shift) % 16
        return e1[(block // 2) * 4 + rem_op(i % 2, a), block % 2]

    def send_e2(d, carry):
        i = (me + d) % 32
        for a in range(2):
            e2s[i, a] = pick_e(i, a)
        remote(e2s.at[i], erem.at[:, own_rows, :], 6, (i // 4, z, i % 4)).start()
        return carry

    lax.fori_loop(1, 32, send_e2, 0)
    for a in range(2):
        erem[a, own_rows, :] = pick_e(me, a)

    arrived(p1, 2)
    own_strip = pl.ds(pl.multiple_of(256 * e + 16 * u, 16), 16)

    def send_p2(d, carry):
        j = (u + d) % 16
        p2s[j] = p1[(j + shift) % 16]
        remote(p2s.at[j], prem.at[:, own_strip, :], 7, (j // 2, z, 2 * (j % 2) + e)).start()
        return carry

    lax.fori_loop(1, 16, send_p2, 0)
    prem[:, own_strip, :] = p1[(u + shift) % 16]

    cross_e.wait_recv()
    from_chip = eloc.at[2 * (1 - c) + e]
    pass_e = remote(from_chip, from_chip, 8, other_core)
    pass_e.start()
    direct_p.wait_recv()
    own_part = pn.at[pl.ds(0, 2), :, half, :]
    pass_p = remote(own_part, own_part, 9, other_core)
    pass_p.start()
    own_e.wait_recv()
    pass_e.wait_recv()
    pass_p.wait_recv()

    pn[2] = -pn[0]
    pn[3] = -pn[1]

    def scalars(code):
        return tab_ref[5 * code], [tab_ref[5 * code + 1 + s] for s in range(4)]

    def times_local(step, carry):
        a, s = step // 4, step % 4
        op = jnp.where(is_a, e + 2 * a, partbuf[e + 2 * a, 0, 0])
        left_re, left_im, right = [], [], []
        for r in range(4):
            code = gam_ref[op, r]
            pattern = tab_ref[5 * code]
            power = tab_ref[5 * code + 1 + s]
            left_re.append(pn[(4 - power) % 4, s ^ pattern])
            left_im.append(pn[(5 - power) % 4, s ^ pattern])
            right.append(
                jnp.concatenate([eloc[op, pl.ds(256 * r, 128), :], eloc[op, pl.ds(256 * r + 128, 128), :]], axis=1)
            )
        right = jnp.concatenate(right, axis=0)
        by_re = jnp.dot(jnp.concatenate(left_re, axis=1), right, preferred_element_type=jnp.float32)
        by_im = jnp.dot(jnp.concatenate(left_im, axis=1), right, preferred_element_type=jnp.float32)
        lanes = pl.ds(pl.multiple_of(128 * s, 128), 128)
        fbuf[a, pl.ds(0, 512), lanes] = (by_re[:, :128] - by_im[:, 128:]).astype(jnp.bfloat16)
        fbuf[a, pl.ds(512, 512), lanes] = (by_re[:, 128:] + by_im[:, :128]).astype(jnp.bfloat16)
        return carry

    lax.fori_loop(0, 8, times_local, 0)

    arrived(e1.at[pl.ds(0, 31)], 6)

    def turn(step, carry):
        rows = pl.ds(pl.multiple_of(128 * (step % 8), 128), 128)
        ptr[step] = erem[step // 8, rows, :].astype(jnp.float32).T
        return carry

    lax.fori_loop(0, 16, turn, 0)

    arrived(p1.at[pl.ds(0, 15)], 7)
    own_rem = prem.at[:, half, :]
    pass_r = remote(own_rem, own_rem, 10, other_core)
    pass_r.start()
    pass_r.wait_recv()

    lane = lax.broadcasted_iota(jnp.int32, (8, 128), 1)
    for a in range(2):

        def times_remote(step, carry):
            cols = pl.ds(pl.multiple_of(256 * step, 256), 256)
            by_re = jnp.dot(fbuf[a], prem[0, :, cols], preferred_element_type=jnp.float32)
            by_im = jnp.dot(fbuf[a], prem[1, :, cols], preferred_element_type=jnp.float32)
            n_re = by_re[:512] - by_im[512:]
            n_im = by_re[512:] + by_im[:512]
            for s in range(2):
                nbuf[0, 2 * step + s] = n_re[:, 128 * s : 128 * s + 128]
                nbuf[1, 2 * step + s] = n_im[:, 128 * s : 128 * s + 128]
            return carry

        lax.fori_loop(0, 2, times_remote, 0)
        op = rem_op(e, a)

        def close(r, carry):
            acc_re, acc_im = carry
            code = gam_ref[op, r]
            pattern = tab_ref[5 * code]
            sum_re = jnp.zeros((128, 128), jnp.float32)
            sum_im = jnp.zeros((128, 128), jnp.float32)
            for s in range(4):
                power = tab_ref[5 * code + 1 + s]
                ca = jnp.where(power == 0, 1.0, jnp.where(power == 2, -1.0, 0.0))
                cb = jnp.where(power == 1, 1.0, jnp.where(power == 3, -1.0, 0.0))
                n_re = nbuf[0, s ^ pattern, pl.ds(128 * s, 128), :]
                n_im = nbuf[1, s ^ pattern, pl.ds(128 * s, 128), :]
                sum_re += ca * n_re - cb * n_im
                sum_im += ca * n_im + cb * n_re
            t_re, t_im = ptr[8 * a + 2 * r], ptr[8 * a + 2 * r + 1]
            return acc_re + sum_re * t_re - sum_im * t_im, acc_im + sum_re * t_im + sum_im * t_re

        zero = jnp.zeros((128, 128), jnp.float32)
        acc_re, acc_im = lax.fori_loop(0, 4, close, (zero, zero))
        res[a] = jnp.where(
            lane == 2 * k, jnp.sum(acc_re) / 512, jnp.where(lane == 2 * k + 1, jnp.sum(acc_im) / 512, 0.0)
        )

    def send_r1(d, carry):
        remote(res, r1.at[z], 11, (src, (z + d) % 8, mom)).start()
        return carry

    lax.fori_loop(1, 8, send_r1, 0)
    r1[z] = res[...]
    arrived(r1.at[pl.ds(0, 7)], 11)
    row = lax.broadcasted_iota(jnp.int32, (8, 128), 0)
    for a in range(2):
        tile = jnp.zeros((8, 128), jnp.float32)
        for plane in range(8):
            tile = jnp.where(row == plane, r1[plane, a], tile)
        t2[a] = tile

    def send_r2(d, carry):
        j = (u + d) % 16
        remote(t2.at[j % 2], r2.at[u], 12, (j // 2, z, 2 * (j % 2) + e)).start()
        return carry

    lax.fori_loop(1, 16, send_r2, 0)
    r2[u] = t2[c]
    arrived(r2.at[pl.ds(0, 15)], 12)

    odd_planes = (row == 0) | (row == 3) | (row == 5) | (row == 6)

    def gather(v, carry):
        even_row = jnp.sum(jnp.where(odd_planes, 0.0, r2[v]), axis=0, keepdims=True)
        tile = jnp.zeros((8, 128), jnp.float32)
        for kk in range(NSEP):
            sep_k = sep_ref[kk]
            block = ((2 * v + 1 + sep_k - ((1 + sep_k) & 1)) // 2) % 16
            tile += jnp.where(row == ROLE_B_PLANES[kk], r2[block], 0.0)
        odd_row = jnp.sum(tile, axis=0, keepdims=True)
        out_ref[v] = jnp.concatenate([even_row, odd_row], axis=0)
        return carry

    lax.fori_loop(0, 16, gather, 0)

    left(partbuf.at[pl.ds(0, 3)], 0)
    left(e1.at[pl.ds(0, 31)], 1)
    left(p1, 2)
    own_e.wait_send()
    cross_e.wait_send()
    direct_p.wait_send()
    left(e1.at[pl.ds(0, 31)], 6)
    left(p1.at[pl.ds(0, 15)], 7)
    pass_e.wait_send()
    pass_p.wait_send()
    pass_r.wait_send()
    left(r1.at[pl.ds(0, 7)], 11)
    left(r2.at[pl.ds(0, 15)], 12)


def shards(peram_blocks, projections, gamma_index, partner, separations):
    bf, f32 = jnp.bfloat16, jnp.float32
    smem = pl.BlockSpec(memory_space=pltpu.SMEM)
    anywhere = pl.BlockSpec(memory_space=pl.ANY)
    out = pl.pallas_call(
        body,
        out_shape=jax.ShapeDtypeStruct((16, 2, 128), f32),
        in_specs=[smem] * 4 + [anywhere] * 2,
        out_specs=pl.BlockSpec(memory_space=pltpu.VMEM),
        scratch_shapes=[
            pltpu.VMEM((4, 1024, 128), bf),
            pltpu.VMEM((2, 2, 256, 512), bf),
            pltpu.VMEM((2, 1024, 128), bf),
            pltpu.VMEM((2, 256, 512), bf),
            pltpu.VMEM((2, 4, 256, 128), bf),
            pltpu.VMEM((1024, 128), bf),
            pltpu.VMEM((32, 2, 32, 128), bf),
            pltpu.VMEM((16, 2, 16, 512), bf),
            pltpu.VMEM((32, 2, 32, 128), bf),
            pltpu.VMEM((16, 2, 16, 512), bf),
            pltpu.VMEM((4, 1024, 128), bf),
            pltpu.VMEM((2, 1024, 128), bf),
            pltpu.VMEM((2, 512, 512), bf),
            pltpu.VMEM((4, 4, 512, 128), bf),
            pltpu.VMEM((2, 1024, 512), bf),
            pltpu.VMEM((2, 4, 512, 128), f32),
            pltpu.VMEM((16, 128, 128), f32),
            pltpu.VMEM((4, 8, 128), jnp.int32),
            pltpu.VMEM((2, 8, 128), f32),
            pltpu.VMEM((8, 2, 8, 128), f32),
            pltpu.VMEM((2, 8, 128), f32),
            pltpu.VMEM((16, 8, 128), f32),
            pltpu.SemaphoreType.DMA((2,)),
            pltpu.SemaphoreType.DMA((13,)),
            pltpu.SemaphoreType.DMA((13,)),
        ],
        compiler_params=pltpu.CompilerParams(has_side_effects=True, vmem_limit_bytes=48 * 1024 * 1024),
    )(
        separations,
        gamma_index,
        partner,
        jnp.asarray(gamma_table()),
        peram_blocks,
        projections.reshape(4, 1024, 128),
    )
    return out[:, :, : 2 * NSEP].reshape(32, NSEP, 1, 2)


def solution(mesh):
    placed = (
        P("src", "snk", None, None, None),
        P("src", "mom", None, None, None, None),
        P(),
        P("mom"),
        P(),
    )
    return jax.shard_map(
        shards, mesh=mesh, in_specs=placed, out_specs=P(None, None, "mom", None), check_vma=False
    )
```

```python
import functools

import jax
import jax.numpy as jnp
import numpy as np
from jax import lax
from jax.experimental import pallas as pl
from jax.experimental.pallas import tpu as pltpu
from jax.sharding import PartitionSpec as P

MESH = pl.DeviceIdType.MESH
NSEP = 4
ROLE_B_PLANES = (6, 3, 0, 5)


def gamma_table():
    unit = np.eye(4, dtype=complex)
    one = np.array([[0, 0, 0, 1j], [0, 0, 1j, 0], [0, -1j, 0, 0], [-1j, 0, 0, 0]])
    two = np.array([[0, 0, 0, -1], [0, 0, 1, 0], [0, 1, 0, 0], [-1, 0, 0, 0]], dtype=complex)
    three = np.array([[0, 0, 1j, 0], [0, 0, 0, -1j], [-1j, 0, 0, 0], [0, 1j, 0, 0]])
    four = np.array([[0, 0, 1, 0], [0, 0, 0, 1], [1, 0, 0, 0], [0, 1, 0, 0]], dtype=complex)
    rows = []
    for code in range(16):
        value = unit
        for position, factor in enumerate((one, two, three, four)):
            if code >> position & 1:
                value = value @ factor
        pattern = int(np.flatnonzero(np.abs(value[:, 0]))[0])
        powers = [(1, 1j, -1, -1j).index(complex(value[s ^ pattern, s])) for s in range(4)]
        rows.append([pattern] + powers)
    return np.array(rows, dtype=np.int32).reshape(-1)


def body(
    sep_hbm, gam_hbm, part_hbm, tab_hbm, p_ref, e_ref, out_ref,
    sep_ref, gam_ref, part_ref, tab_ref,
    e_in, p_in, e_snd, p_snd, pl_snd, el_snd, e1, p1_re, p1_im, e2s, p2s, eloc, erem, prem, pn,
    fbuf, nbuf, ptr, partbuf, res, r1, t2, r2, lsem, ssem, rsem,
):
    src, z, mom = lax.axis_index("src"), lax.axis_index("snk"), lax.axis_index("mom")
    c, e = mom // 2, mom % 2
    u = 2 * src + c
    me = 4 * src + mom
    k = (z + 2) % 4
    z_even = 1 - z % 2
    z_rem = (z + 2 + 4 * z_even) % 8
    z_loc = (z + 6 + 4 * z_even) % 8

    def remote(src_ref, dst_ref, index, target):
        return pltpu.make_async_remote_copy(
            src_ref=src_ref, dst_ref=dst_ref, send_sem=ssem.at[index], recv_sem=rsem.at[index],
            device_id=target, device_id_type=MESH,
        )

    def arrived(ref, index):
        pltpu.make_async_copy(ref, ref, rsem.at[index]).wait()

    def left(ref, index):
        pltpu.make_async_copy(ref, ref, ssem.at[index]).wait()

    p1 = (p1_re, p1_im)
    other_core = (src, z, 2 * c + 1 - e)
    other_chip = (src, z, 2 * (1 - c) + e)
    half = pl.ds(pl.multiple_of(256 * e, 256), 256)
    own_rows = pl.ds(pl.multiple_of(32 * me, 32), 32)
    own_strip = pl.ds(pl.multiple_of(256 * e + 16 * u, 16), 16)

    loads = [
        pltpu.make_async_copy(one, two, lsem.at[index])
        for index, (one, two) in enumerate(
            (
                (part_hbm, part_ref),
                (sep_hbm, sep_ref),
                (gam_hbm, gam_ref),
                (tab_hbm, tab_ref),
                (e_ref, e_in),
                (p_ref.at[pl.ds(2 * c, 2), 0, :, half, :], p_in),
            )
        )
    ]
    for load in loads:
        load.start()

    barrier = pltpu.get_barrier_semaphore()

    def greet(target):
        pl.semaphore_signal(barrier, inc=1, device_id=target, device_id_type=MESH)

    def greet_blocks(d, carry):
        j = (u + d) % 16
        greet((j // 2, z_loc, 2 * (j % 2) + e))
        return carry

    def greet_plane(d, carry):
        i = (me + d) % 32
        greet((i // 4, z, i % 4))
        return carry

    lax.fori_loop(0, 16, greet_blocks, 0)
    greet((src, z_rem, mom))
    for d in (1, 3, 4, 5, 7):
        greet((src, (z + d) % 8, mom))
    lax.fori_loop(1, 32, greet_plane, 0)

    for load in loads[:5]:
        load.wait()
    sep = sep_ref[k]
    odd = sep & 1
    is_a = (z + z // 2 + z // 4) % 2 == 1
    shift = jnp.where(is_a, sep >> 1, 16 - ((sep + 1) >> 1))
    par_loc = jnp.where(is_a, 0, (1 + odd) & 1)
    par_rem = jnp.where(is_a, odd, 1)
    odd_own = sep_ref[z % 4] & 1
    snd_rem = jnp.where(z < NSEP, 1, odd_own)
    snd_loc = jnp.where(z < NSEP, 0, (1 + odd_own) & 1)
    partbuf[mom] = jnp.full((8, 128), part_ref[0], jnp.int32)
    for h in range(2):
        e_snd[h] = e_in[2 * h + par_rem]
    loads[5].wait()
    p_snd[...] = p_in[snd_rem]

    pl.semaphore_wait(barrier, 53)

    def send_partner(d, carry):
        remote(partbuf.at[mom], partbuf.at[mom], 0, (src, z, (mom + d) % 4)).start()
        return carry

    lax.fori_loop(1, 4, send_partner, 0)

    def send_e1(d, carry):
        i = (me + d) % 32
        rows = pl.ds(pl.multiple_of(32 * i, 32), 32)
        remote(e_snd.at[:, rows, :], e1.at[me], 1, (i // 4, z, i % 4)).start()
        return carry

    lax.fori_loop(1, 32, send_e1, 0)
    e1[me] = e_snd[:, own_rows, :]

    for plane in range(2):

        def send_p1(d, carry):
            j = (u + d) % 16
            rows = pl.ds(pl.multiple_of(16 * j, 16), 16)
            remote(
                p_snd.at[plane, rows, :], p1[plane].at[u], 2 + plane, (j // 2, z_rem, 2 * (j % 2) + e)
            ).start()
            return carry

        lax.fori_loop(0, 16, send_p1, 0)

    eloc[mom] = e_in[2 * c + par_loc]
    own_e = remote(eloc.at[mom], eloc.at[mom], 4, other_core)
    own_e.start()
    el_snd[...] = e_in[2 * (1 - c) + par_loc]
    for s in range(4):
        pl_snd[:, s] = p_in[snd_loc, :, :, pl.ds(128 * s, 128)]

    arrived(partbuf.at[pl.ds(0, 3)], 0)
    partners = [partbuf[o, 0, 0] for o in range(4)]
    arrived(e1.at[pl.ds(0, 31)], 1)

    def rem_op(core, a):
        return jnp.where(is_a, jnp.where(core == 0, partners[2 * a], partners[2 * a + 1]), core + 2 * a)

    def pick_e(i, a):
        block = (i // 2 + shift) % 16
        return e1[(block // 2) * 4 + rem_op(i % 2, a), block % 2]

    def send_e2(d, carry):
        i = (me + d) % 32
        for a in range(2):
            e2s[i, a] = pick_e(i, a)
        remote(e2s.at[i], erem.at[:, own_rows, :], 5, (i // 4, z, i % 4)).start()
        return carry

    lax.fori_loop(1, 32, send_e2, 0)
    for a in range(2):
        erem[a, own_rows, :] = pick_e(me, a)

    direct_p = remote(pl_snd, pn.at[pl.ds(0, 2), :, half, :], 6, (src, z_loc, mom))
    direct_p.start()
    cross_e = remote(el_snd, eloc.at[mom], 7, other_chip)
    cross_e.start()

    for plane in range(2):
        arrived(p1[plane], 2 + plane)

        def send_p2(d, carry):
            j = (u + d) % 16
            p2s[plane, j] = p1[plane][(j + shift) % 16]
            remote(
                p2s.at[plane, j], prem.at[plane, own_strip, :], 8 + plane, (j // 2, z, 2 * (j % 2) + e)
            ).start()
            return carry

        lax.fori_loop(1, 16, send_p2, 0)
        prem[plane, own_strip, :] = p1[plane][(u + shift) % 16]

    cross_e.wait_recv()
    from_chip = eloc.at[2 * (1 - c) + e]
    pass_e = remote(from_chip, from_chip, 10, other_core)
    pass_e.start()
    direct_p.wait_recv()
    own_part = pn.at[pl.ds(0, 2), :, half, :]
    pass_p = remote(own_part, own_part, 11, other_core)
    pass_p.start()
    own_e.wait_recv()
    pass_e.wait_recv()
    pass_p.wait_recv()

    pn[2] = -pn[0]
    pn[3] = -pn[1]

    def times_local(step, carry):
        a, s = step // 4, step % 4
        op = jnp.where(is_a, e + 2 * a, partbuf[e + 2 * a, 0, 0])
        left_re, left_im, right = [], [], []
        for r in range(4):
            code = gam_ref[op, r]
            pattern = tab_ref[5 * code]
            power = tab_ref[5 * code + 1 + s]
            left_re.append(pn[(4 - power) % 4, s ^ pattern])
            left_im.append(pn[(5 - power) % 4, s ^ pattern])
            right.append(
                jnp.concatenate([eloc[op, pl.ds(256 * r, 128), :], eloc[op, pl.ds(256 * r + 128, 128), :]], axis=1)
            )
        right = jnp.concatenate(right, axis=0)
        by_re = jnp.dot(jnp.concatenate(left_re, axis=1), right, preferred_element_type=jnp.float32)
        by_im = jnp.dot(jnp.concatenate(left_im, axis=1), right, preferred_element_type=jnp.float32)
        lanes = pl.ds(pl.multiple_of(128 * s, 128), 128)
        fbuf[a, pl.ds(0, 512), lanes] = (by_re[:, :128] - by_im[:, 128:]).astype(jnp.bfloat16)
        fbuf[a, pl.ds(512, 512), lanes] = (by_re[:, 128:] + by_im[:, :128]).astype(jnp.bfloat16)
        return carry

    lax.fori_loop(0, 8, times_local, 0)

    arrived(e1.at[pl.ds(0, 31)], 5)

    def turn(step, carry):
        rows = pl.ds(pl.multiple_of(128 * (step % 8), 128), 128)
        ptr[step] = erem[step // 8, rows, :].astype(jnp.float32).T
        return carry

    lax.fori_loop(0, 16, turn, 0)

    passes = []
    for plane in range(2):
        arrived(p1[plane].at[pl.ds(0, 15)], 8 + plane)
        own_rem = prem.at[plane, half, :]
        passes.append(remote(own_rem, own_rem, 12 + plane, other_core))
        passes[plane].start()
        passes[plane].wait_recv()

        def times_remote(step, carry):
            a, cols = step // 2, pl.ds(pl.multiple_of(256 * (step % 2), 256), 256)
            product = jnp.dot(fbuf[a], prem[plane, :, cols], preferred_element_type=jnp.float32)
            for s in range(2):
                lanes = slice(128 * s, 128 * s + 128)
                spin = 2 * (step % 2) + s
                if plane == 0:
                    nbuf[a, 0, spin] = product[:512, lanes]
                    nbuf[a, 1, spin] = product[512:, lanes]
                else:
                    nbuf[a, 0, spin] -= product[512:, lanes]
                    nbuf[a, 1, spin] += product[:512, lanes]
            return carry

        lax.fori_loop(0, 4, times_remote, 0)

    lane = lax.broadcasted_iota(jnp.int32, (8, 128), 1)
    for a in range(2):
        op = rem_op(e, a)

        def close(r, carry):
            acc_re, acc_im = carry
            code = gam_ref[op, r]
            pattern = tab_ref[5 * code]
            sum_re = jnp.zeros((128, 128), jnp.float32)
            sum_im = jnp.zeros((128, 128), jnp.float32)
            for s in range(4):
                power = tab_ref[5 * code + 1 + s]
                ca = jnp.where(power == 0, 1.0, jnp.where(power == 2, -1.0, 0.0))
                cb = jnp.where(power == 1, 1.0, jnp.where(power == 3, -1.0, 0.0))
                n_re = nbuf[a, 0, s ^ pattern, pl.ds(128 * s, 128), :]
                n_im = nbuf[a, 1, s ^ pattern, pl.ds(128 * s, 128), :]
                sum_re += ca * n_re - cb * n_im
                sum_im += ca * n_im + cb * n_re
            t_re, t_im = ptr[8 * a + 2 * r], ptr[8 * a + 2 * r + 1]
            return acc_re + sum_re * t_re - sum_im * t_im, acc_im + sum_re * t_im + sum_im * t_re

        zero = jnp.zeros((128, 128), jnp.float32)
        acc_re, acc_im = lax.fori_loop(0, 4, close, (zero, zero))
        res[a] = jnp.where(
            lane == 2 * k, jnp.sum(acc_re) / 512, jnp.where(lane == 2 * k + 1, jnp.sum(acc_im) / 512, 0.0)
        )

    def send_r1(d, carry):
        remote(res, r1.at[z], 14, (src, (z + d) % 8, mom)).start()
        return carry

    lax.fori_loop(1, 8, send_r1, 0)
    r1[z] = res[...]
    arrived(r1.at[pl.ds(0, 7)], 14)
    row = lax.broadcasted_iota(jnp.int32, (8, 128), 0)
    for a in range(2):
        tile = jnp.zeros((8, 128), jnp.float32)
        for plane in range(8):
            tile = jnp.where(row == plane, r1[plane, a], tile)
        t2[a] = tile

    def send_r2(d, carry):
        j = (u + d) % 16
        remote(t2.at[j % 2], r2.at[u], 15, (j // 2, z, 2 * (j % 2) + e)).start()
        return carry

    lax.fori_loop(1, 16, send_r2, 0)
    r2[u] = t2[c]
    arrived(r2.at[pl.ds(0, 15)], 15)

    odd_planes = (row == 0) | (row == 3) | (row == 5) | (row == 6)

    def gather(v, carry):
        even_row = jnp.sum(jnp.where(odd_planes, 0.0, r2[v]), axis=0, keepdims=True)
        tile = jnp.zeros((8, 128), jnp.float32)
        for kk in range(NSEP):
            sep_k = sep_ref[kk]
            block = ((2 * v + 1 + sep_k - ((1 + sep_k) & 1)) // 2) % 16
            tile += jnp.where(row == ROLE_B_PLANES[kk], r2[block], 0.0)
        odd_row = jnp.sum(tile, axis=0, keepdims=True)
        out_ref[v] = jnp.concatenate([even_row, odd_row], axis=0)
        return carry

    lax.fori_loop(0, 16, gather, 0)

    left(partbuf.at[pl.ds(0, 3)], 0)
    left(e1.at[pl.ds(0, 31)], 1)
    left(e1.at[pl.ds(0, 31)], 5)
    for plane in range(2):
        left(p1[plane], 2 + plane)
        left(p1[plane].at[pl.ds(0, 15)], 8 + plane)
    for copy in [own_e, cross_e, direct_p, pass_e, pass_p] + passes:
        copy.wait_send()
    left(r1.at[pl.ds(0, 7)], 14)
    left(r2.at[pl.ds(0, 15)], 15)


def shards(peram_blocks, projections, gamma_index, partner, separations):
    bf, f32 = jnp.bfloat16, jnp.float32
    anywhere = pl.BlockSpec(memory_space=pl.ANY)
    out = pl.pallas_call(
        body,
        out_shape=jax.ShapeDtypeStruct((16, 2, 128), f32),
        in_specs=[anywhere] * 6,
        out_specs=pl.BlockSpec(memory_space=pltpu.VMEM),
        scratch_shapes=[
            pltpu.SMEM((4,), jnp.int32),
            pltpu.SMEM((4, 4), jnp.int32),
            pltpu.SMEM((1,), jnp.int32),
            pltpu.SMEM((80,), jnp.int32),
            pltpu.VMEM((4, 1024, 128), bf),
            pltpu.VMEM((2, 2, 256, 512), bf),
            pltpu.VMEM((2, 1024, 128), bf),
            pltpu.VMEM((2, 256, 512), bf),
            pltpu.VMEM((2, 4, 256, 128), bf),
            pltpu.VMEM((1024, 128), bf),
            pltpu.VMEM((32, 2, 32, 128), bf),
            pltpu.VMEM((16, 16, 512), bf),
            pltpu.VMEM((16, 16, 512), bf),
            pltpu.VMEM((32, 2, 32, 128), bf),
            pltpu.VMEM((2, 16, 16, 512), bf),
            pltpu.VMEM((4, 1024, 128), bf),
            pltpu.VMEM((2, 1024, 128), bf),
            pltpu.VMEM((2, 512, 512), bf),
            pltpu.VMEM((4, 4, 512, 128), bf),
            pltpu.VMEM((2, 1024, 512), bf),
            pltpu.VMEM((2, 2, 4, 512, 128), f32),
            pltpu.VMEM((16, 128, 128), f32),
            pltpu.VMEM((4, 8, 128), jnp.int32),
            pltpu.VMEM((2, 8, 128), f32),
            pltpu.VMEM((8, 2, 8, 128), f32),
            pltpu.VMEM((2, 8, 128), f32),
            pltpu.VMEM((16, 8, 128), f32),
            pltpu.SemaphoreType.DMA((6,)),
            pltpu.SemaphoreType.DMA((16,)),
            pltpu.SemaphoreType.DMA((16,)),
        ],
        compiler_params=pltpu.CompilerParams(collective_id=0, has_side_effects=True, vmem_limit_bytes=48 * 1024 * 1024),
    )(
        separations,
        gamma_index,
        partner,
        jnp.asarray(gamma_table()),
        peram_blocks,
        projections.reshape(4, 1024, 128),
    )
    return out[:, :, : 2 * NSEP].reshape(32, NSEP, 1, 2)


def solution(mesh):
    placed = (
        P("src", "snk", None, None, None),
        P("src", "mom", None, None, None, None),
        P(),
        P("mom"),
        P(),
    )
    return jax.shard_map(
        shards, mesh=mesh, in_specs=placed, out_specs=P(None, None, "mom", None), check_vma=False
    )
```

```python
import functools

import jax
import jax.numpy as jnp
import numpy as np
from jax import lax
from jax.experimental import pallas as pl
from jax.experimental.pallas import tpu as pltpu
from jax.sharding import PartitionSpec as P

MESH = pl.DeviceIdType.MESH
NSEP = 4
ROLE_B_PLANES = (6, 3, 0, 5)


def gamma_table():
    unit = np.eye(4, dtype=complex)
    one = np.array([[0, 0, 0, 1j], [0, 0, 1j, 0], [0, -1j, 0, 0], [-1j, 0, 0, 0]])
    two = np.array([[0, 0, 0, -1], [0, 0, 1, 0], [0, 1, 0, 0], [-1, 0, 0, 0]], dtype=complex)
    three = np.array([[0, 0, 1j, 0], [0, 0, 0, -1j], [-1j, 0, 0, 0], [0, 1j, 0, 0]])
    four = np.array([[0, 0, 1, 0], [0, 0, 0, 1], [1, 0, 0, 0], [0, 1, 0, 0]], dtype=complex)
    rows = []
    for code in range(16):
        value = unit
        for position, factor in enumerate((one, two, three, four)):
            if code >> position & 1:
                value = value @ factor
        pattern = int(np.flatnonzero(np.abs(value[:, 0]))[0])
        powers = [(1, 1j, -1, -1j).index(complex(value[s ^ pattern, s])) for s in range(4)]
        rows.append([pattern] + powers)
    return np.array(rows, dtype=np.int32).reshape(-1)


def body(
    sep_hbm, gam_hbm, part_hbm, tab_hbm, p_ref, e_ref, out_ref,
    sep_ref, gam_ref, part_ref, tab_ref,
    e_in, p_in, e_snd, p_snd, pl_snd, el_snd, e1, p1_re, p1_im, e2s, p2s, eloc, erem, ploc, pmine, pother,
    fbuf, nbuf, ptr, partbuf, res, r1, t2, r2, lsem, ssem, rsem,
):
    src, z, mom = lax.axis_index("src"), lax.axis_index("snk"), lax.axis_index("mom")
    c, e = mom // 2, mom % 2
    u = 2 * src + c
    me = 4 * src + mom
    k = (z + 2) % 4
    z_even = 1 - z % 2
    z_rem = (z + 2 + 4 * z_even) % 8
    z_loc = (z + 6 + 4 * z_even) % 8

    def remote(src_ref, dst_ref, index, target):
        return pltpu.make_async_remote_copy(
            src_ref=src_ref, dst_ref=dst_ref, send_sem=ssem.at[index], recv_sem=rsem.at[index],
            device_id=target, device_id_type=MESH,
        )

    def arrived(ref, index):
        pltpu.make_async_copy(ref, ref, rsem.at[index]).wait()

    def left(ref, index):
        pltpu.make_async_copy(ref, ref, ssem.at[index]).wait()

    p1 = (p1_re, p1_im)
    other_core = (src, z, 2 * c + 1 - e)
    other_chip = (src, z, 2 * (1 - c) + e)
    half = pl.ds(pl.multiple_of(256 * e, 256), 256)
    own_rows = pl.ds(pl.multiple_of(32 * me, 32), 32)
    own_strip = pl.ds(pl.multiple_of(16 * u, 16), 16)

    loads = [
        pltpu.make_async_copy(one, two, lsem.at[index])
        for index, (one, two) in enumerate(
            (
                (part_hbm, part_ref),
                (sep_hbm, sep_ref),
                (gam_hbm, gam_ref),
                (tab_hbm, tab_ref),
                (e_ref, e_in),
                (p_ref.at[pl.ds(2 * c, 2), 0, :, half, :], p_in),
            )
        )
    ]
    for load in loads:
        load.start()

    barrier = pltpu.get_barrier_semaphore()

    def greet(target):
        pl.semaphore_signal(barrier, inc=1, device_id=target, device_id_type=MESH)

    def greet_blocks(d, carry):
        j = (u + d) % 16
        greet((j // 2, z_loc, 2 * (j % 2) + e))
        return carry

    def greet_plane(d, carry):
        i = (me + d) % 32
        greet((i // 4, z, i % 4))
        return carry

    lax.fori_loop(0, 16, greet_blocks, 0)
    greet((src, z_rem, mom))
    for d in (1, 3, 4, 5, 7):
        greet((src, (z + d) % 8, mom))
    lax.fori_loop(1, 32, greet_plane, 0)

    for load in loads[:5]:
        load.wait()
    sep = sep_ref[k]
    odd = sep & 1
    is_a = (z + z // 2 + z // 4) % 2 == 1
    shift = jnp.where(is_a, sep >> 1, 16 - ((sep + 1) >> 1))
    par_loc = jnp.where(is_a, 0, (1 + odd) & 1)
    par_rem = jnp.where(is_a, odd, 1)
    odd_own = sep_ref[z % 4] & 1
    snd_rem = jnp.where(z < NSEP, 1, odd_own)
    snd_loc = jnp.where(z < NSEP, 0, (1 + odd_own) & 1)
    partbuf[mom] = jnp.full((8, 128), part_ref[0], jnp.int32)
    for h in range(2):
        e_snd[h] = e_in[2 * h + par_rem]
    loads[5].wait()
    for s in range(4):
        p_snd[:, s] = p_in[snd_rem, :, :, pl.ds(128 * s, 128)]

    pl.semaphore_wait(barrier, 53)

    def send_partner(d, carry):
        remote(partbuf.at[mom], partbuf.at[mom], 0, (src, z, (mom + d) % 4)).start()
        return carry

    lax.fori_loop(1, 4, send_partner, 0)

    def send_e1(d, carry):
        i = (me + d) % 32
        rows = pl.ds(pl.multiple_of(32 * i, 32), 32)
        remote(e_snd.at[:, rows, :], e1.at[me], 1, (i // 4, z, i % 4)).start()
        return carry

    lax.fori_loop(1, 32, send_e1, 0)
    e1[me] = e_snd[:, own_rows, :]

    for plane in range(2):

        def send_p1(d, carry):
            j = (u + d) % 16
            rows = pl.ds(pl.multiple_of(16 * j, 16), 16)
            remote(
                p_snd.at[plane, :, rows, :], p1[plane].at[u], 2 + plane, (j // 2, z_rem, 2 * (j % 2) + e)
            ).start()
            return carry

        lax.fori_loop(0, 16, send_p1, 0)

    eloc[mom] = e_in[2 * c + par_loc]
    own_e = remote(eloc.at[mom], eloc.at[mom], 4, other_core)
    own_e.start()
    el_snd[...] = e_in[2 * (1 - c) + par_loc]
    pl_snd[...] = p_in[snd_loc]

    arrived(partbuf.at[pl.ds(0, 3)], 0)
    partners = [partbuf[o, 0, 0] for o in range(4)]
    arrived(e1.at[pl.ds(0, 31)], 1)

    def rem_op(core, a):
        return jnp.where(is_a, jnp.where(core == 0, partners[2 * a], partners[2 * a + 1]), core + 2 * a)

    def pick_e(i, a):
        block = (i // 2 + shift) % 16
        return e1[(block // 2) * 4 + rem_op(i % 2, a), block % 2]

    def send_e2(d, carry):
        i = (me + d) % 32
        for a in range(2):
            e2s[i, a] = pick_e(i, a)
        remote(e2s.at[i], erem.at[:, own_rows, :], 5, (i // 4, z, i % 4)).start()
        return carry

    lax.fori_loop(1, 32, send_e2, 0)
    for a in range(2):
        erem[a, own_rows, :] = pick_e(me, a)

    cross_e = remote(el_snd, eloc.at[mom], 7, other_chip)
    cross_e.start()
    chunks = [pl.ds(pl.multiple_of(256 * e + 128 * i, 128), 128) for i in range(2)]
    direct_p = []
    for i in range(2):
        part = pl_snd.at[:, pl.ds(128 * i, 128), :]
        direct_p.append(remote(part, ploc.at[:, chunks[i], :], 16 + i, (src, z_loc, mom)))
        direct_p[i].start()

    for plane in range(2):
        arrived(p1[plane], 2 + plane)

        def send_p2(d, carry):
            j = (u + d) % 16
            p2s[plane, j] = p1[plane][(j + shift) % 16]
            remote(
                p2s.at[plane, j], pmine.at[plane, :, own_strip, :], 8 + plane, (j // 2, z, 2 * (j % 2) + e)
            ).start()
            return carry

        lax.fori_loop(1, 16, send_p2, 0)
        pmine[plane, :, own_strip, :] = p1[plane][(u + shift) % 16]

    cross_e.wait_recv()
    from_chip = eloc.at[2 * (1 - c) + e]
    pass_e = remote(from_chip, from_chip, 10, other_core)
    pass_e.start()
    pass_p, pass_r = [], []

    def pass_local(i):
        direct_p[i].wait_recv()
        part = ploc.at[:, chunks[i], :]
        pass_p.append(remote(part, part, 11 + i, other_core))
        pass_p[i].start()

    pass_local(0)
    own_e.wait_recv()
    pass_e.wait_recv()

    def loc_op(a):
        return jnp.where(is_a, e + 2 * a, partbuf[e + 2 * a, 0, 0])

    def turn(step, carry):
        rows = pl.ds(pl.multiple_of(128 * (step % 8), 128), 128)
        ptr[step] = eloc[loc_op(step // 8), rows, :].astype(jnp.float32).T
        return carry

    lax.fori_loop(0, 16, turn, 0)

    arrived(e1.at[pl.ds(0, 31)], 5)
    for plane in range(2):
        arrived(p1[plane].at[pl.ds(0, 15)], 8 + plane)
        pass_r.append(remote(pmine.at[plane], pother.at[plane], 18 + plane, other_core))
        pass_r[plane].start()

    def times_projections(block, which):
        block[2] = -block[0]
        block[3] = -block[1]

        def product(step, carry):
            a, s = step // 4, step % 4
            own_rem_op = jnp.where(is_a, partbuf[e + 2 * a, 0, 0], e + 2 * a)
            left_re, left_im, right = [], [], []
            for r in range(4):
                code = gam_ref[own_rem_op, r]
                pattern = tab_ref[5 * code]
                power = tab_ref[5 * code + 1 + s]
                left_re.append(block[(4 - power) % 4, s ^ pattern])
                left_im.append(block[(5 - power) % 4, s ^ pattern])
                right.append(
                    jnp.concatenate([erem[a, pl.ds(256 * r, 128), :], erem[a, pl.ds(256 * r + 128, 128), :]], axis=1)
                )
            left = jnp.concatenate([jnp.concatenate(left_re, axis=1), jnp.concatenate(left_im, axis=1)], axis=0)
            both = jnp.dot(left, jnp.concatenate(right, axis=0), preferred_element_type=jnp.float32)
            lanes = pl.ds(pl.multiple_of(128 * s, 128), 128)
            re_rows = pl.ds(pl.multiple_of(256 * which, 256), 256)
            im_rows = pl.ds(pl.multiple_of(256 * which + 512, 256), 256)
            fbuf[a, re_rows, lanes] = (both[:256, :128] - both[256:, 128:]).astype(jnp.bfloat16)
            fbuf[a, im_rows, lanes] = (both[:256, 128:] + both[256:, :128]).astype(jnp.bfloat16)
            return carry

        lax.fori_loop(0, 8, product, 0)

    times_projections(pmine, e)
    pass_local(1)
    for copy in pass_r:
        copy.wait_recv()
    times_projections(pother, 1 - e)

    for i in range(2):
        pass_p[i].wait_recv()

        def times_local(step, carry):
            a, cols = step // 2, pl.ds(pl.multiple_of(256 * (step % 2), 256), 256)
            left = jnp.concatenate([fbuf[a, :, pl.ds(128 * i, 128)], fbuf[a, :, pl.ds(256 + 128 * i, 128)]], axis=1)
            by = []
            for plane in range(2):
                right = jnp.concatenate(
                    [ploc[plane, pl.ds(128 * i, 128), cols], ploc[plane, pl.ds(256 + 128 * i, 128), cols]], axis=0
                )
                by.append(jnp.dot(left, right, preferred_element_type=jnp.float32))
            n_re = by[0][:512] - by[1][512:]
            n_im = by[0][512:] + by[1][:512]
            for s in range(2):
                lanes = slice(128 * s, 128 * s + 128)
                spin = 2 * (step % 2) + s
                if i == 0:
                    nbuf[a, 0, spin] = n_re[:, lanes]
                    nbuf[a, 1, spin] = n_im[:, lanes]
                else:
                    nbuf[a, 0, spin] += n_re[:, lanes]
                    nbuf[a, 1, spin] += n_im[:, lanes]
            return carry

        lax.fori_loop(0, 4, times_local, 0)

    lane = lax.broadcasted_iota(jnp.int32, (8, 128), 1)
    for a in range(2):
        op = loc_op(a)

        def close(r, carry):
            acc_re, acc_im = carry
            code = gam_ref[op, r]
            pattern = tab_ref[5 * code]
            sum_re = jnp.zeros((128, 128), jnp.float32)
            sum_im = jnp.zeros((128, 128), jnp.float32)
            for s in range(4):
                power = tab_ref[5 * code + 1 + s]
                ca = jnp.where(power == 0, 1.0, jnp.where(power == 2, -1.0, 0.0))
                cb = jnp.where(power == 1, 1.0, jnp.where(power == 3, -1.0, 0.0))
                n_re = nbuf[a, 0, s ^ pattern, pl.ds(128 * s, 128), :]
                n_im = nbuf[a, 1, s ^ pattern, pl.ds(128 * s, 128), :]
                sum_re += ca * n_re - cb * n_im
                sum_im += ca * n_im + cb * n_re
            t_re, t_im = ptr[8 * a + 2 * r], ptr[8 * a + 2 * r + 1]
            return acc_re + sum_re * t_re - sum_im * t_im, acc_im + sum_re * t_im + sum_im * t_re

        zero = jnp.zeros((128, 128), jnp.float32)
        acc_re, acc_im = lax.fori_loop(0, 4, close, (zero, zero))
        res[a] = jnp.where(
            lane == 2 * k, jnp.sum(acc_re) / 512, jnp.where(lane == 2 * k + 1, jnp.sum(acc_im) / 512, 0.0)
        )

    def send_r1(d, carry):
        remote(res, r1.at[z], 14, (src, (z + d) % 8, mom)).start()
        return carry

    lax.fori_loop(1, 8, send_r1, 0)
    r1[z] = res[...]
    arrived(r1.at[pl.ds(0, 7)], 14)
    row = lax.broadcasted_iota(jnp.int32, (8, 128), 0)
    for a in range(2):
        tile = jnp.zeros((8, 128), jnp.float32)
        for plane in range(8):
            tile = jnp.where(row == plane, r1[plane, a], tile)
        t2[a] = tile

    def send_r2(d, carry):
        j = (u + d) % 16
        remote(t2.at[j % 2], r2.at[u], 15, (j // 2, z, 2 * (j % 2) + e)).start()
        return carry

    lax.fori_loop(1, 16, send_r2, 0)
    r2[u] = t2[c]
    arrived(r2.at[pl.ds(0, 15)], 15)

    odd_planes = (row == 0) | (row == 3) | (row == 5) | (row == 6)

    def gather(v, carry):
        even_row = jnp.sum(jnp.where(odd_planes, 0.0, r2[v]), axis=0, keepdims=True)
        tile = jnp.zeros((8, 128), jnp.float32)
        for kk in range(NSEP):
            sep_k = sep_ref[kk]
            block = ((2 * v + 1 + sep_k - ((1 + sep_k) & 1)) // 2) % 16
            tile += jnp.where(row == ROLE_B_PLANES[kk], r2[block], 0.0)
        odd_row = jnp.sum(tile, axis=0, keepdims=True)
        out_ref[v] = jnp.concatenate([even_row, odd_row], axis=0)
        return carry

    lax.fori_loop(0, 16, gather, 0)

    left(partbuf.at[pl.ds(0, 3)], 0)
    left(e1.at[pl.ds(0, 31)], 1)
    left(e1.at[pl.ds(0, 31)], 5)
    for plane in range(2):
        left(p1[plane], 2 + plane)
        left(p1[plane].at[pl.ds(0, 15)], 8 + plane)
    for copy in [own_e, cross_e, pass_e] + direct_p + pass_p + pass_r:
        copy.wait_send()
    left(r1.at[pl.ds(0, 7)], 14)
    left(r2.at[pl.ds(0, 15)], 15)


def shards(peram_blocks, projections, gamma_index, partner, separations):
    bf, f32 = jnp.bfloat16, jnp.float32
    anywhere = pl.BlockSpec(memory_space=pltpu.HBM)
    out = pl.pallas_call(
        body,
        out_shape=jax.ShapeDtypeStruct((16, 2, 128), f32),
        in_specs=[anywhere] * 6,
        out_specs=pl.BlockSpec(memory_space=pltpu.VMEM),
        scratch_shapes=[
            pltpu.SMEM((4,), jnp.int32),
            pltpu.SMEM((4, 4), jnp.int32),
            pltpu.SMEM((1,), jnp.int32),
            pltpu.SMEM((80,), jnp.int32),
            pltpu.VMEM((4, 1024, 128), bf),
            pltpu.VMEM((2, 2, 256, 512), bf),
            pltpu.VMEM((2, 1024, 128), bf),
            pltpu.VMEM((2, 4, 256, 128), bf),
            pltpu.VMEM((2, 256, 512), bf),
            pltpu.VMEM((1024, 128), bf),
            pltpu.VMEM((32, 2, 32, 128), bf),
            pltpu.VMEM((16, 4, 16, 128), bf),
            pltpu.VMEM((16, 4, 16, 128), bf),
            pltpu.VMEM((32, 2, 32, 128), bf),
            pltpu.VMEM((2, 16, 4, 16, 128), bf),
            pltpu.VMEM((4, 1024, 128), bf),
            pltpu.VMEM((2, 1024, 128), bf),
            pltpu.VMEM((2, 512, 512), bf),
            pltpu.VMEM((4, 4, 256, 128), bf),
            pltpu.VMEM((4, 4, 256, 128), bf),
            pltpu.VMEM((2, 1024, 512), bf),
            pltpu.VMEM((2, 2, 4, 512, 128), f32),
            pltpu.VMEM((16, 128, 128), f32),
            pltpu.VMEM((4, 8, 128), jnp.int32),
            pltpu.VMEM((2, 8, 128), f32),
            pltpu.VMEM((8, 2, 8, 128), f32),
            pltpu.VMEM((2, 8, 128), f32),
            pltpu.VMEM((16, 8, 128), f32),
            pltpu.SemaphoreType.DMA((6,)),
            pltpu.SemaphoreType.DMA((20,)),
            pltpu.SemaphoreType.DMA((20,)),
        ],
        compiler_params=pltpu.CompilerParams(collective_id=0, has_side_effects=True, vmem_limit_bytes=64 * 1024 * 1024 - 65536),
    )(
        separations,
        gamma_index,
        partner,
        jnp.asarray(gamma_table()),
        peram_blocks,
        projections.reshape(4, 1024, 128),
    )
    return out[:, :, : 2 * NSEP].reshape(32, NSEP, 1, 2)


def solution(mesh):
    placed = (
        P("src", "snk", None, None, None),
        P("src", "mom", None, None, None, None),
        P(),
        P("mom"),
        P(),
    )
    return jax.shard_map(
        shards, mesh=mesh, in_specs=placed, out_specs=P(None, None, "mom", None), check_vma=False
    )
```

```python
import functools

import jax
import jax.numpy as jnp
import numpy as np
from jax import lax
from jax.experimental import pallas as pl
from jax.experimental.pallas import tpu as pltpu
from jax.sharding import PartitionSpec as P

MESH = pl.DeviceIdType.MESH
NSEP = 4


def gamma_table():
    unit = np.eye(4, dtype=complex)
    one = np.array([[0, 0, 0, 1j], [0, 0, 1j, 0], [0, -1j, 0, 0], [-1j, 0, 0, 0]])
    two = np.array([[0, 0, 0, -1], [0, 0, 1, 0], [0, 1, 0, 0], [-1, 0, 0, 0]], dtype=complex)
    three = np.array([[0, 0, 1j, 0], [0, 0, 0, -1j], [-1j, 0, 0, 0], [0, 1j, 0, 0]])
    four = np.array([[0, 0, 1, 0], [0, 0, 0, 1], [1, 0, 0, 0], [0, 1, 0, 0]], dtype=complex)
    rows = []
    for code in range(16):
        value = unit
        for position, factor in enumerate((one, two, three, four)):
            if code >> position & 1:
                value = value @ factor
        pattern = int(np.flatnonzero(np.abs(value[:, 0]))[0])
        powers = [(1, 1j, -1, -1j).index(complex(value[s ^ pattern, s])) for s in range(4)]
        rows.append([pattern] + powers)
    return np.array(rows, dtype=np.int32).reshape(-1)


def body(
    sep_hbm, gam_hbm, part_hbm, tab_hbm, p_ref, e_ref, out_ref,
    sep_ref, gam_ref, part_ref, tab_ref,
    e_in, p_in, e_snd, p_snd, pl_snd, el_snd, e1, p1_re, p1_im, e2s, p2s, eloc, erem_0, erem_1, ploc, pmine, pother,
    fbuf, ptr, elt, partbuf, res, r1, t2, r2, lsem, ssem, rsem,
):
    src, z, mom = lax.axis_index("src"), lax.axis_index("snk"), lax.axis_index("mom")
    c, e = mom >> 1, mom & 1
    u = 2 * src + c
    me = 4 * src + mom
    k = (z + 2) & 3
    z_even = 1 - (z & 1)
    z_rem = (z + 2 + 4 * z_even) & 7
    z_loc = (z + 6 + 4 * z_even) & 7
    p1 = (p1_re, p1_im)
    erem = (erem_0, erem_1)

    def remote(src_ref, dst_ref, index, target):
        return pltpu.make_async_remote_copy(
            src_ref=src_ref, dst_ref=dst_ref, send_sem=ssem.at[index], recv_sem=rsem.at[index],
            device_id=target, device_id_type=MESH,
        )

    def arrived(ref, index):
        pltpu.make_async_copy(ref, ref, rsem.at[index]).wait()

    def left(ref, index):
        pltpu.make_async_copy(ref, ref, ssem.at[index]).wait()

    def near(d):
        flip = (d >> 2) & 1
        column = ((src >> 1) + d) & 3
        return 2 * column + ((src & 1) ^ flip), c ^ flip

    other_core = (src, z, 2 * c + 1 - e)
    other_chip = (src, z, 2 * (1 - c) + e)
    half = pl.ds(pl.multiple_of(256 * e, 256), 256)
    own_rows = pl.ds(pl.multiple_of(32 * me, 32), 32)
    own_strip = pl.ds(pl.multiple_of(16 * u, 16), 16)

    loads = [
        pltpu.make_async_copy(one, two, lsem.at[index])
        for index, (one, two) in enumerate(
            (
                (part_hbm, part_ref),
                (sep_hbm, sep_ref),
                (gam_hbm, gam_ref),
                (tab_hbm, tab_ref),
                (e_ref, e_in),
                (p_ref.at[:, 0, :, half, :], p_in),
            )
        )
    ]
    for load in loads:
        load.start()

    barrier = pltpu.get_barrier_semaphore()

    def greet(target):
        pl.semaphore_signal(barrier, inc=1, device_id=target, device_id_type=MESH)

    def greet_blocks(d, carry):
        there, chip = near(d)
        greet((there, z_loc, 2 * chip + e))
        return carry

    def greet_plane(d, carry):
        i = (me + d) & 31
        greet((i >> 2, z, i & 3))
        return carry

    lax.fori_loop(0, 8, greet_blocks, 0)
    greet((src, z_rem, mom))
    for d in (1, 3, 4, 5, 7):
        greet((src, (z + d) & 7, mom))
    lax.fori_loop(1, 32, greet_plane, 0)

    for load in loads[:5]:
        load.wait()
    sep = sep_ref[k]
    odd = sep & 1
    is_a = ((z + (z >> 1) + (z >> 2)) & 1) == 1
    shift = jnp.where(is_a, sep >> 1, 16 - ((sep + 1) >> 1))
    par_loc = jnp.where(is_a, 0, (1 + odd) & 1)
    par_rem = jnp.where(is_a, odd, 1)
    time = (2 * u + jnp.where(is_a, 0, par_loc - sep)) & 31
    odd_own = sep_ref[z & 3] & 1
    snd_rem = jnp.where(z < NSEP, 1, odd_own)
    snd_loc = jnp.where(z < NSEP, 0, (1 + odd_own) & 1)
    partbuf[mom] = jnp.full((8, 128), part_ref[0], jnp.int32)
    for h in range(2):
        e_snd[h] = e_in[2 * h + par_rem]
    eloc[mom] = e_in[2 * c + par_loc]
    el_snd[...] = e_in[2 * (1 - c) + par_loc]
    loads[5].wait()
    for h in range(2):
        for s in range(4):
            p_snd[:, h, s] = p_in[2 * h + snd_rem, :, :, pl.ds(128 * s, 128)]
    pl_snd[...] = p_in[2 * c + snd_loc]

    pl.semaphore_wait(barrier, 45)

    def send_partner(d, carry):
        remote(partbuf.at[mom], partbuf.at[mom], 0, (src, z, (mom + d) & 3)).start()
        return carry

    lax.fori_loop(1, 4, send_partner, 0)

    def send_e1(d, carry):
        i = (me + d) & 31
        rows = pl.ds(pl.multiple_of(32 * i, 32), 32)
        remote(e_snd.at[:, rows, :], e1.at[me], 1, (i >> 2, z, i & 3)).start()
        return carry

    lax.fori_loop(1, 32, send_e1, 0)

    for plane in range(2):

        def send_p1(d, carry):
            there, chip = near(d)
            rows = pl.ds(pl.multiple_of(16 * (2 * there + chip), 16), 16)
            h = d >> 3
            remote(
                p_snd.at[plane, h, :, rows, :], p1[plane].at[2 * src + h], 2 + plane, (there, z_rem, 2 * chip + e)
            ).start()
            return carry

        lax.fori_loop(0, 16, send_p1, 0)

    own_e = remote(eloc.at[mom], eloc.at[mom], 4, other_core)
    own_e.start()
    cross_e = remote(el_snd, eloc.at[mom], 7, other_chip)
    cross_e.start()
    e1[me] = e_snd[:, own_rows, :]

    arrived(partbuf.at[pl.ds(0, 3)], 0)
    partners = [partbuf[o, 0, 0] for o in range(4)]
    arrived(e1.at[pl.ds(0, 31)], 1)

    def pick_e(i, a):
        block = ((i >> 1) + shift) & 15
        op = jnp.where(is_a, jnp.where((i & 1) == 0, partners[2 * a], partners[2 * a + 1]), (i & 1) + 2 * a)
        return e1[(block >> 1) * 4 + op, block & 1]

    def spread_e2(a):
        def send_e2(d, carry):
            i = (me + d) & 31
            e2s[a, i] = pick_e(i, a)
            remote(e2s.at[a, i], erem[a].at[own_rows, :], 5 + a, (i >> 2, z, i & 3)).start()
            return carry

        lax.fori_loop(1, 32, send_e2, 0)
        erem[a][own_rows, :] = pick_e(me, a)

    spread_e2(0)

    chunks = [pl.ds(pl.multiple_of(256 * e + 128 * i, 128), 128) for i in range(2)]
    direct_p = []
    for i in range(2):
        part = pl_snd.at[:, pl.ds(128 * i, 128), :]
        direct_p.append(remote(part, ploc.at[:, chunks[i], :], 17 + i, (src, z_loc, mom)))
        direct_p[i].start()

    for plane in range(2):
        arrived(p1[plane], 2 + plane)

        def send_p2(d, carry):
            j = (u + d) & 15
            p2s[plane, j] = p1[plane][(j + shift) & 15]
            remote(
                p2s.at[plane, j], pmine.at[plane, :, own_strip, :], 8 + plane, (j >> 1, z, 2 * (j & 1) + e)
            ).start()
            return carry

        lax.fori_loop(1, 16, send_p2, 0)
        pmine[plane, :, own_strip, :] = p1[plane][(u + shift) & 15]
    spread_e2(1)

    cross_e.wait_recv()
    from_chip = eloc.at[2 * (1 - c) + e]
    pass_e = remote(from_chip, from_chip, 10, other_core)
    pass_e.start()
    pass_p, pass_r = [], []

    def pass_local(i):
        direct_p[i].wait_recv()
        part = ploc.at[:, chunks[i], :]
        pass_p.append(remote(part, part, 11 + i, other_core))
        pass_p[i].start()

    own_e.wait_recv()
    pass_e.wait_recv()

    def loc_op(a):
        return jnp.where(is_a, e + 2 * a, partbuf[e + 2 * a, 0, 0])

    def turn(step, carry):
        rows = pl.ds(pl.multiple_of(128 * (step & 7), 128), 128)
        ptr[step] = eloc[loc_op(step >> 3), rows, :].astype(jnp.float32).T
        return carry

    lax.fori_loop(0, 16, turn, 0)

    def build(step, carry):
        a, s = step >> 2, step & 3
        op = loc_op(a)
        sum_re = [jnp.zeros((128, 128), jnp.float32) for _ in range(4)]
        sum_im = [jnp.zeros((128, 128), jnp.float32) for _ in range(4)]
        for r in range(4):
            code = gam_ref[op, r]
            pattern = tab_ref[5 * code]
            power = tab_ref[5 * code + 1 + s]
            ca = jnp.where(power == 0, 1.0, jnp.where(power == 2, -1.0, 0.0))
            cb = jnp.where(power == 1, 1.0, jnp.where(power == 3, -1.0, 0.0))
            t_re, t_im = ptr[8 * a + 2 * r], ptr[8 * a + 2 * r + 1]
            v_re = ca * t_re - cb * t_im
            v_im = ca * t_im + cb * t_re
            for s_left in range(4):
                here = jnp.where((s ^ pattern) == s_left, 1.0, 0.0)
                sum_re[s_left] += here * v_re
                sum_im[s_left] += here * v_im
        rows = pl.ds(pl.multiple_of(128 * s, 128), 128)
        for s_left in range(4):
            elt[a, 0, rows, pl.ds(128 * s_left, 128)] = sum_re[s_left]
            elt[a, 1, rows, pl.ds(128 * s_left, 128)] = sum_im[s_left]
        return carry

    lax.fori_loop(0, 8, build, 0)

    pass_local(0)
    for plane in range(2):
        arrived(p1[plane].at[pl.ds(0, 15)], 8 + plane)
        pass_r.append(remote(pmine.at[plane], pother.at[plane], 13 + plane, other_core))
        pass_r[plane].start()

    def negate(block):
        block[2] = -block[0]
        block[3] = -block[1]

    def times_projections(block, which, a):
        op = jnp.where(is_a, partbuf[e + 2 * a, 0, 0], e + 2 * a)
        right = jnp.concatenate(
            [
                jnp.concatenate([erem[a][pl.ds(256 * r, 128), :], erem[a][pl.ds(256 * r + 128, 128), :]], axis=1)
                for r in range(4)
            ],
            axis=0,
        )
        re_rows = pl.ds(pl.multiple_of(256 * which, 256), 256)
        im_rows = pl.ds(pl.multiple_of(256 * which + 512, 256), 256)
        for s in range(4):
            left_re, left_im = [], []
            for r in range(4):
                code = gam_ref[op, r]
                pattern = tab_ref[5 * code]
                power = tab_ref[5 * code + 1 + s]
                left_re.append(block[(4 - power) & 3, s ^ pattern])
                left_im.append(block[(5 - power) & 3, s ^ pattern])
            by_re = jnp.dot(jnp.concatenate(left_re, axis=1), right, preferred_element_type=jnp.float32)
            by_im = jnp.dot(jnp.concatenate(left_im, axis=1), right, preferred_element_type=jnp.float32)
            lanes = pl.ds(128 * s, 128)
            fbuf[a, re_rows, lanes] = (by_re[:, :128] - by_im[:, 128:]).astype(jnp.bfloat16)
            fbuf[a, im_rows, lanes] = (by_re[:, 128:] + by_im[:, :128]).astype(jnp.bfloat16)

    lane = lax.broadcasted_iota(jnp.int32, (8, 128), 1)
    row = lax.broadcasted_iota(jnp.int32, (8, 128), 0)

    def close(a):
        def times_local(step, carry):
            acc_re, acc_im = carry
            cols = pl.ds(pl.multiple_of(256 * step, 256), 256)
            by_re = jnp.dot(fbuf[a], ploc[0, :, cols], preferred_element_type=jnp.float32)
            by_im = jnp.dot(fbuf[a], ploc[1, :, cols], preferred_element_type=jnp.float32)
            n_re = by_re[:512] - by_im[512:]
            n_im = by_re[512:] + by_im[:512]
            t_re, t_im = elt[a, 0, :, cols], elt[a, 1, :, cols]
            new_re = n_re * t_re - n_im * t_im
            new_im = n_re * t_im + n_im * t_re
            return (
                acc_re + jnp.sum(new_re.reshape(64, 8, 256), axis=0),
                acc_im + jnp.sum(new_im.reshape(64, 8, 256), axis=0),
            )

        zero = jnp.zeros((8, 256), jnp.float32)
        acc_re, acc_im = lax.fori_loop(0, 2, times_local, (zero, zero))
        mine = jnp.where(row == 2 * k, jnp.sum(acc_re) / 512, jnp.where(row == 2 * k + 1, jnp.sum(acc_im) / 512, 0.0))
        res[a] = jnp.where(lane == time, mine, 0.0)

    arrived(e1.at[pl.ds(0, 31), 0], 5)
    negate(pmine)
    times_projections(pmine, e, 0)
    pass_local(1)
    for copy in pass_r:
        copy.wait_recv()
    negate(pother)
    times_projections(pother, 1 - e, 0)
    for copy in pass_p:
        copy.wait_recv()
    close(0)
    arrived(e1.at[pl.ds(0, 31), 0], 6)
    times_projections(pmine, e, 1)
    times_projections(pother, 1 - e, 1)
    close(1)

    def send_r1(d, carry):
        remote(res, r1.at[z], 15, (src, (z + d) & 7, mom)).start()
        return carry

    lax.fori_loop(1, 8, send_r1, 0)
    r1[z] = res[...]
    arrived(r1.at[pl.ds(0, 7)], 15)
    t2[...] = jnp.sum(r1[...], axis=0)

    def send_r2(d, carry):
        j = (u + d) & 15
        remote(t2.at[j & 1], r2.at[u], 16, (j >> 1, z, 2 * (j & 1) + e)).start()
        return carry

    lax.fori_loop(1, 16, send_r2, 0)
    r2[u] = t2[c]
    arrived(r2.at[pl.ds(0, 15)], 16)
    total = jnp.sum(r2[...], axis=0)
    for kk in range(NSEP):
        out_ref[kk, 0] = total[2 * kk : 2 * kk + 2, :32]

    left(partbuf.at[pl.ds(0, 3)], 0)
    left(e1.at[pl.ds(0, 31)], 1)
    for a in range(2):
        left(e1.at[pl.ds(0, 31), 0], 5 + a)
    for plane in range(2):
        left(p1[plane], 2 + plane)
        left(p1[plane].at[pl.ds(0, 15)], 8 + plane)
    for copy in [own_e, cross_e, pass_e] + direct_p + pass_p + pass_r:
        copy.wait_send()
    left(r1.at[pl.ds(0, 7)], 15)
    left(r2.at[pl.ds(0, 15)], 16)


def shards(peram_blocks, projections, gamma_index, partner, separations):
    bf, f32, i32 = jnp.bfloat16, jnp.float32, jnp.int32
    buffers = [
        ((4, 1024, 128), bf),
        ((4, 2, 256, 512), bf),
        ((2, 1024, 128), bf),
        ((2, 2, 4, 256, 128), bf),
        ((2, 256, 512), bf),
        ((1024, 128), bf),
        ((32, 2, 32, 128), bf),
        ((16, 4, 16, 128), bf),
        ((16, 4, 16, 128), bf),
        ((2, 32, 32, 128), bf),
        ((2, 16, 4, 16, 128), bf),
        ((4, 1024, 128), bf),
        ((1024, 128), bf),
        ((1024, 128), bf),
        ((2, 512, 512), bf),
        ((4, 4, 256, 128), bf),
        ((4, 4, 256, 128), bf),
        ((2, 1024, 512), bf),
        ((16, 128, 128), f32),
        ((2, 2, 512, 512), f32),
        ((4, 8, 128), i32),
        ((2, 8, 128), f32),
        ((8, 2, 8, 128), f32),
        ((2, 8, 128), f32),
        ((16, 8, 128), f32),
    ]
    out = pl.pallas_call(
        body,
        out_shape=jax.ShapeDtypeStruct((NSEP, 1, 2, 32), f32),
        in_specs=[pl.BlockSpec(memory_space=pltpu.HBM)] * 6,
        out_specs=pl.BlockSpec(memory_space=pltpu.VMEM),
        scratch_shapes=[pltpu.SMEM(shape, i32) for shape in ((4,), (4, 4), (1,), (80,))]
        + [pltpu.VMEM(shape, dtype) for shape, dtype in buffers]
        + [pltpu.SemaphoreType.DMA((count,)) for count in (6, 19, 19)],
        compiler_params=pltpu.CompilerParams(
            collective_id=0, has_side_effects=True, vmem_limit_bytes=64 * 1024 * 1024 - 65536
        ),
    )(
        separations,
        gamma_index,
        partner,
        jnp.asarray(gamma_table()),
        peram_blocks,
        projections.reshape(4, 1024, 128),
    )
    return jnp.transpose(out, (3, 0, 1, 2))


def solution(mesh):
    placed = (
        P("src", "snk", None, None, None),
        P("src", "mom", None, None, None, None),
        P(),
        P("mom"),
        P(),
    )
    return jax.shard_map(
        shards, mesh=mesh, in_specs=placed, out_specs=P(None, None, "mom", None), check_vma=False
    )
```

```python
import functools

import jax
import jax.numpy as jnp
import numpy as np
from jax import lax
from jax.experimental import pallas as pl
from jax.experimental.pallas import tpu as pltpu
from jax.sharding import PartitionSpec as P

MESH = pl.DeviceIdType.MESH
NSEP = 4


def gamma_table():
    unit = np.eye(4, dtype=complex)
    one = np.array([[0, 0, 0, 1j], [0, 0, 1j, 0], [0, -1j, 0, 0], [-1j, 0, 0, 0]])
    two = np.array([[0, 0, 0, -1], [0, 0, 1, 0], [0, 1, 0, 0], [-1, 0, 0, 0]], dtype=complex)
    three = np.array([[0, 0, 1j, 0], [0, 0, 0, -1j], [-1j, 0, 0, 0], [0, 1j, 0, 0]])
    four = np.array([[0, 0, 1, 0], [0, 0, 0, 1], [1, 0, 0, 0], [0, 1, 0, 0]], dtype=complex)
    rows = []
    for code in range(16):
        value = unit
        for position, factor in enumerate((one, two, three, four)):
            if code >> position & 1:
                value = value @ factor
        pattern = int(np.flatnonzero(np.abs(value[:, 0]))[0])
        powers = [(1, 1j, -1, -1j).index(complex(value[s ^ pattern, s])) for s in range(4)]
        rows.append([pattern] + powers)
    return np.array(rows, dtype=np.int32).reshape(-1)


def body(
    sep_hbm, gam_hbm, part_hbm, tab_hbm, p_ref, e_ref, out_ref,
    sep_ref, gam_ref, part_ref, tab_ref,
    e_in, p_in, e_snd, p_snd, pl_snd, el_snd, e1, p1_re, p1_im, e2s, p2s, eloc, erem_0, erem_1, ploc, pmine, pother,
    fbuf, ptr, elt, partbuf, res, r1, t2, r2, lsem, ssem, rsem,
):
    src, z, mom = lax.axis_index("src"), lax.axis_index("snk"), lax.axis_index("mom")
    c, e = mom >> 1, mom & 1
    u = 2 * src + c
    me = 4 * src + mom
    k = (z + 2) & 3
    z_even = 1 - (z & 1)
    z_rem = (z + 2 + 4 * z_even) & 7
    z_loc = (z + 6 + 4 * z_even) & 7
    p1 = (p1_re, p1_im)
    erem = (erem_0, erem_1)

    def remote(src_ref, dst_ref, index, target):
        return pltpu.make_async_remote_copy(
            src_ref=src_ref, dst_ref=dst_ref, send_sem=ssem.at[index], recv_sem=rsem.at[index],
            device_id=target, device_id_type=MESH,
        )

    def arrived(ref, index):
        pltpu.make_async_copy(ref, ref, rsem.at[index]).wait()

    def left(ref, index):
        pltpu.make_async_copy(ref, ref, ssem.at[index]).wait()

    def near(d):
        flip = (d >> 2) & 1
        column = ((src >> 1) + d) & 3
        return 2 * column + ((src & 1) ^ flip), c ^ flip

    other_core = (src, z, 2 * c + 1 - e)
    other_chip = (src, z, 2 * (1 - c) + e)
    half = pl.ds(pl.multiple_of(256 * e, 256), 256)
    own_rows = pl.ds(pl.multiple_of(32 * me, 32), 32)
    own_strip = pl.ds(pl.multiple_of(16 * u, 16), 16)

    loads = [
        pltpu.make_async_copy(one, two, lsem.at[index])
        for index, (one, two) in enumerate(
            (
                (part_hbm, part_ref),
                (sep_hbm, sep_ref),
                (gam_hbm, gam_ref),
                (tab_hbm, tab_ref),
                (e_ref, e_in),
                (p_ref.at[:, 0, :, half, :], p_in),
            )
        )
    ]
    for load in loads:
        load.start()

    barrier = pltpu.get_barrier_semaphore()

    def greet(target):
        pl.semaphore_signal(barrier, inc=1, device_id=target, device_id_type=MESH)

    def greet_blocks(d, carry):
        there, chip = near(d)
        greet((there, z_loc, 2 * chip + e))
        return carry

    def greet_plane(d, carry):
        i = (me + d) & 31
        greet((i >> 2, z, i & 3))
        return carry

    lax.fori_loop(0, 8, greet_blocks, 0)
    greet((src, z_rem, mom))
    for d in (1, 3, 4, 5, 7):
        greet((src, (z + d) & 7, mom))
    lax.fori_loop(1, 32, greet_plane, 0)

    for load in loads[:5]:
        load.wait()
    sep = sep_ref[k]
    odd = sep & 1
    is_a = ((z + (z >> 1) + (z >> 2)) & 1) == 1
    shift = jnp.where(is_a, sep >> 1, 16 - ((sep + 1) >> 1))
    par_loc = jnp.where(is_a, 0, (1 + odd) & 1)
    par_rem = jnp.where(is_a, odd, 1)
    time = (2 * u + jnp.where(is_a, 0, par_loc - sep)) & 31
    odd_own = sep_ref[z & 3] & 1
    snd_rem = jnp.where(z < NSEP, 1, odd_own)
    snd_loc = jnp.where(z < NSEP, 0, (1 + odd_own) & 1)
    partbuf[mom] = jnp.full((8, 128), part_ref[0], jnp.int32)
    for h in range(2):
        e_snd[h] = e_in[2 * h + par_rem]
    eloc[mom] = e_in[2 * c + par_loc]
    el_snd[...] = e_in[2 * (1 - c) + par_loc]
    loads[5].wait()
    for h in range(2):
        for s in range(4):
            p_snd[:, h, s] = p_in[2 * h + snd_rem, :, :, pl.ds(128 * s, 128)]
    pl_snd[...] = p_in[2 * c + snd_loc]

    pl.semaphore_wait(barrier, 45)

    def send_partner(d, carry):
        remote(partbuf.at[mom], partbuf.at[mom], 0, (src, z, (mom + d) & 3)).start()
        return carry

    lax.fori_loop(1, 4, send_partner, 0)

    def spread_p1(plane):
        def send_p1(d, carry):
            there, chip = near(d)
            rows = pl.ds(pl.multiple_of(16 * (2 * there + chip), 16), 16)
            h = d >> 3
            remote(
                p_snd.at[plane, h, :, rows, :], p1[plane].at[2 * src + h], 2 + plane, (there, z_rem, 2 * chip + e)
            ).start()
            return carry

        lax.fori_loop(0, 16, send_p1, 0)

    spread_p1(0)

    def send_e1(d, carry):
        i = (me + d) & 31
        rows = pl.ds(pl.multiple_of(32 * i, 32), 32)
        remote(e_snd.at[:, rows, :], e1.at[me], 1, (i >> 2, z, i & 3)).start()
        return carry

    lax.fori_loop(1, 32, send_e1, 0)

    spread_p1(1)

    own_e = remote(eloc.at[mom], eloc.at[mom], 4, other_core)
    own_e.start()
    cross_e = remote(el_snd, eloc.at[mom], 7, other_chip)
    cross_e.start()
    e1[me] = e_snd[:, own_rows, :]

    chunks = [pl.ds(pl.multiple_of(256 * e + 128 * i, 128), 128) for i in range(2)]
    direct_p = []
    for i in range(2):
        part = pl_snd.at[:, pl.ds(128 * i, 128), :]
        direct_p.append(remote(part, ploc.at[:, chunks[i], :], 17 + i, (src, z_loc, mom)))

    arrived(partbuf.at[pl.ds(0, 3)], 0)
    partners = [partbuf[o, 0, 0] for o in range(4)]
    arrived(e1.at[pl.ds(0, 31)], 1)

    def pick_e(i, a):
        block = ((i >> 1) + shift) & 15
        op = jnp.where(is_a, jnp.where((i & 1) == 0, partners[2 * a], partners[2 * a + 1]), (i & 1) + 2 * a)
        return e1[(block >> 1) * 4 + op, block & 1]

    def spread_e2(a):
        def send_e2(d, carry):
            i = (me + d) & 31
            e2s[a, i] = pick_e(i, a)
            remote(e2s.at[a, i], erem[a].at[own_rows, :], 5 + a, (i >> 2, z, i & 3)).start()
            return carry

        lax.fori_loop(1, 32, send_e2, 0)
        erem[a][own_rows, :] = pick_e(me, a)

    spread_e2(0)

    spread_e2(1)
    for plane in range(2):
        arrived(p1[plane], 2 + plane)

        def send_p2(d, carry):
            j = (u + d) & 15
            p2s[plane, j] = p1[plane][(j + shift) & 15]
            remote(
                p2s.at[plane, j], pmine.at[plane, :, own_strip, :], 8 + plane, (j >> 1, z, 2 * (j & 1) + e)
            ).start()
            return carry

        lax.fori_loop(1, 16, send_p2, 0)
        pmine[plane, :, own_strip, :] = p1[plane][(u + shift) & 15]
    direct_p[0].start()
    direct_p[1].start()
    cross_e.wait_recv()
    from_chip = eloc.at[2 * (1 - c) + e]
    pass_e = remote(from_chip, from_chip, 10, other_core)
    pass_e.start()
    pass_p, pass_r = [], []

    def pass_local(i):
        direct_p[i].wait_recv()
        part = ploc.at[:, chunks[i], :]
        pass_p.append(remote(part, part, 11 + i, other_core))
        pass_p[i].start()

    own_e.wait_recv()
    pass_e.wait_recv()

    def loc_op(a):
        return jnp.where(is_a, e + 2 * a, partbuf[e + 2 * a, 0, 0])

    def turn(step, carry):
        rows = pl.ds(pl.multiple_of(128 * (step & 7), 128), 128)
        ptr[step] = eloc[loc_op(step >> 3), rows, :].astype(jnp.float32).T
        return carry

    lax.fori_loop(0, 16, turn, 0)

    def build(step, carry):
        a, s = step >> 2, step & 3
        op = loc_op(a)
        sum_re = [jnp.zeros((128, 128), jnp.float32) for _ in range(4)]
        sum_im = [jnp.zeros((128, 128), jnp.float32) for _ in range(4)]
        for r in range(4):
            code = gam_ref[op, r]
            pattern = tab_ref[5 * code]
            power = tab_ref[5 * code + 1 + s]
            ca = jnp.where(power == 0, 1.0, jnp.where(power == 2, -1.0, 0.0))
            cb = jnp.where(power == 1, 1.0, jnp.where(power == 3, -1.0, 0.0))
            t_re, t_im = ptr[8 * a + 2 * r], ptr[8 * a + 2 * r + 1]
            v_re = ca * t_re - cb * t_im
            v_im = ca * t_im + cb * t_re
            for s_left in range(4):
                here = jnp.where((s ^ pattern) == s_left, 1.0, 0.0)
                sum_re[s_left] += here * v_re
                sum_im[s_left] += here * v_im
        rows = pl.ds(pl.multiple_of(128 * s, 128), 128)
        for s_left in range(4):
            elt[a, 0, rows, pl.ds(128 * s_left, 128)] = sum_re[s_left]
            elt[a, 1, rows, pl.ds(128 * s_left, 128)] = sum_im[s_left]
        return carry

    lax.fori_loop(0, 8, build, 0)

    pass_local(0)
    for plane in range(2):
        arrived(p1[plane].at[pl.ds(0, 15)], 8 + plane)
        pass_r.append(remote(pmine.at[plane], pother.at[plane], 13 + plane, other_core))
        pass_r[plane].start()

    def negate(block):
        block[2] = -block[0]
        block[3] = -block[1]

    def times_projections(block, which, a):
        op = jnp.where(is_a, partbuf[e + 2 * a, 0, 0], e + 2 * a)
        right = jnp.concatenate(
            [
                jnp.concatenate([erem[a][pl.ds(256 * r, 128), :], erem[a][pl.ds(256 * r + 128, 128), :]], axis=1)
                for r in range(4)
            ],
            axis=0,
        )
        re_rows = pl.ds(pl.multiple_of(256 * which, 256), 256)
        im_rows = pl.ds(pl.multiple_of(256 * which + 512, 256), 256)
        for s in range(4):
            left_re, left_im = [], []
            for r in range(4):
                code = gam_ref[op, r]
                pattern = tab_ref[5 * code]
                power = tab_ref[5 * code + 1 + s]
                left_re.append(block[(4 - power) & 3, s ^ pattern])
                left_im.append(block[(5 - power) & 3, s ^ pattern])
            by_re = jnp.dot(jnp.concatenate(left_re, axis=1), right, preferred_element_type=jnp.float32)
            by_im = jnp.dot(jnp.concatenate(left_im, axis=1), right, preferred_element_type=jnp.float32)
            lanes = pl.ds(128 * s, 128)
            fbuf[a, re_rows, lanes] = (by_re[:, :128] - by_im[:, 128:]).astype(jnp.bfloat16)
            fbuf[a, im_rows, lanes] = (by_re[:, 128:] + by_im[:, :128]).astype(jnp.bfloat16)

    lane = lax.broadcasted_iota(jnp.int32, (8, 128), 1)
    row = lax.broadcasted_iota(jnp.int32, (8, 128), 0)

    def close(a):
        def times_local(step, carry):
            acc_re, acc_im = carry
            cols = pl.ds(pl.multiple_of(256 * step, 256), 256)
            by_re = jnp.dot(fbuf[a], ploc[0, :, cols], preferred_element_type=jnp.float32)
            by_im = jnp.dot(fbuf[a], ploc[1, :, cols], preferred_element_type=jnp.float32)
            n_re = by_re[:512] - by_im[512:]
            n_im = by_re[512:] + by_im[:512]
            t_re, t_im = elt[a, 0, :, cols], elt[a, 1, :, cols]
            new_re = n_re * t_re - n_im * t_im
            new_im = n_re * t_im + n_im * t_re
            return (
                acc_re + jnp.sum(new_re.reshape(64, 8, 256), axis=0),
                acc_im + jnp.sum(new_im.reshape(64, 8, 256), axis=0),
            )

        zero = jnp.zeros((8, 256), jnp.float32)
        acc_re, acc_im = lax.fori_loop(0, 2, times_local, (zero, zero))
        mine = jnp.where(row == 2 * k, jnp.sum(acc_re) / 512, jnp.where(row == 2 * k + 1, jnp.sum(acc_im) / 512, 0.0))
        res[a] = jnp.where(lane == time, mine, 0.0)

    arrived(e1.at[pl.ds(0, 31), 0], 5)
    negate(pmine)
    times_projections(pmine, e, 0)
    pass_local(1)
    for copy in pass_r:
        copy.wait_recv()
    negate(pother)
    times_projections(pother, 1 - e, 0)
    for copy in pass_p:
        copy.wait_recv()
    close(0)
    arrived(e1.at[pl.ds(0, 31), 0], 6)
    times_projections(pmine, e, 1)
    times_projections(pother, 1 - e, 1)
    close(1)

    def send_r1(d, carry):
        remote(res, r1.at[z], 15, (src, (z + d) & 7, mom)).start()
        return carry

    lax.fori_loop(1, 8, send_r1, 0)
    r1[z] = res[...]
    arrived(r1.at[pl.ds(0, 7)], 15)
    t2[...] = jnp.sum(r1[...], axis=0)

    def send_r2(d, carry):
        j = (u + d) & 15
        remote(t2.at[j & 1], r2.at[u], 16, (j >> 1, z, 2 * (j & 1) + e)).start()
        return carry

    lax.fori_loop(1, 16, send_r2, 0)
    r2[u] = t2[c]
    arrived(r2.at[pl.ds(0, 15)], 16)
    total = jnp.sum(r2[...], axis=0)
    for kk in range(NSEP):
        out_ref[kk, 0] = total[2 * kk : 2 * kk + 2, :32]

    left(partbuf.at[pl.ds(0, 3)], 0)
    left(e1.at[pl.ds(0, 31)], 1)
    for a in range(2):
        left(e1.at[pl.ds(0, 31), 0], 5 + a)
    for plane in range(2):
        left(p1[plane], 2 + plane)
        left(p1[plane].at[pl.ds(0, 15)], 8 + plane)
    for copy in [own_e, cross_e, pass_e] + direct_p + pass_p + pass_r:
        copy.wait_send()
    left(r1.at[pl.ds(0, 7)], 15)
    left(r2.at[pl.ds(0, 15)], 16)


def shards(peram_blocks, projections, gamma_index, partner, separations):
    bf, f32, i32 = jnp.bfloat16, jnp.float32, jnp.int32
    buffers = [
        ((4, 1024, 128), bf),
        ((4, 2, 256, 512), bf),
        ((2, 1024, 128), bf),
        ((2, 2, 4, 256, 128), bf),
        ((2, 256, 512), bf),
        ((1024, 128), bf),
        ((32, 2, 32, 128), bf),
        ((16, 4, 16, 128), bf),
        ((16, 4, 16, 128), bf),
        ((2, 32, 32, 128), bf),
        ((2, 16, 4, 16, 128), bf),
        ((4, 1024, 128), bf),
        ((1024, 128), bf),
        ((1024, 128), bf),
        ((2, 512, 512), bf),
        ((4, 4, 256, 128), bf),
        ((4, 4, 256, 128), bf),
        ((2, 1024, 512), bf),
        ((16, 128, 128), f32),
        ((2, 2, 512, 512), f32),
        ((4, 8, 128), i32),
        ((2, 8, 128), f32),
        ((8, 2, 8, 128), f32),
        ((2, 8, 128), f32),
        ((16, 8, 128), f32),
    ]
    out = pl.pallas_call(
        body,
        out_shape=jax.ShapeDtypeStruct((NSEP, 1, 2, 32), f32),
        in_specs=[pl.BlockSpec(memory_space=pltpu.HBM)] * 6,
        out_specs=pl.BlockSpec(memory_space=pltpu.VMEM),
        scratch_shapes=[pltpu.SMEM(shape, i32) for shape in ((4,), (4, 4), (1,), (80,))]
        + [pltpu.VMEM(shape, dtype) for shape, dtype in buffers]
        + [pltpu.SemaphoreType.DMA((count,)) for count in (6, 19, 19)],
        compiler_params=pltpu.CompilerParams(
            collective_id=0, has_side_effects=True, vmem_limit_bytes=64 * 1024 * 1024 - 65536
        ),
    )(
        separations,
        gamma_index,
        partner,
        jnp.asarray(gamma_table()),
        peram_blocks,
        projections.reshape(4, 1024, 128),
    )
    return jnp.transpose(out, (3, 0, 1, 2))


def solution(mesh):
    placed = (
        P("src", "snk", None, None, None),
        P("src", "mom", None, None, None, None),
        P(),
        P("mom"),
        P(),
    )
    return jax.shard_map(
        shards, mesh=mesh, in_specs=placed, out_specs=P(None, None, "mom", None), check_vma=False
    )
```

```python
import functools

import jax
import jax.numpy as jnp
import numpy as np
from jax import lax
from jax.experimental import pallas as pl
from jax.experimental.pallas import tpu as pltpu
from jax.sharding import PartitionSpec as P

MESH = pl.DeviceIdType.MESH
NSEP = 4


def gamma_table():
    unit = np.eye(4, dtype=complex)
    one = np.array([[0, 0, 0, 1j], [0, 0, 1j, 0], [0, -1j, 0, 0], [-1j, 0, 0, 0]])
    two = np.array([[0, 0, 0, -1], [0, 0, 1, 0], [0, 1, 0, 0], [-1, 0, 0, 0]], dtype=complex)
    three = np.array([[0, 0, 1j, 0], [0, 0, 0, -1j], [-1j, 0, 0, 0], [0, 1j, 0, 0]])
    four = np.array([[0, 0, 1, 0], [0, 0, 0, 1], [1, 0, 0, 0], [0, 1, 0, 0]], dtype=complex)
    rows = []
    for code in range(16):
        value = unit
        for position, factor in enumerate((one, two, three, four)):
            if code >> position & 1:
                value = value @ factor
        pattern = int(np.flatnonzero(np.abs(value[:, 0]))[0])
        powers = [(1, 1j, -1, -1j).index(complex(value[s ^ pattern, s])) for s in range(4)]
        rows.append([pattern] + powers)
    return np.array(rows, dtype=np.int32).reshape(-1)


def body(
    sep_hbm, gam_hbm, part_hbm, tab_hbm, p_ref, e_ref, out_ref,
    sep_ref, gam_ref, part_ref, tab_ref,
    e_in, p_in, e_snd, p_snd, pl_snd, el_snd, e1_0, e1_1, p1_re, p1_im, e2s, p2s, eloc, erem, ploc, pmine, pother,
    bacc, ptr, elt, erd, partbuf, res, r1, t2, r2, lsem, ssem, rsem,
):
    src, z, mom = lax.axis_index("src"), lax.axis_index("snk"), lax.axis_index("mom")
    c, e = mom >> 1, mom & 1
    u = 2 * src + c
    me = 4 * src + mom
    k = (z + 2) & 3
    z_even = 1 - (z & 1)
    z_rem = (z + 2 + 4 * z_even) & 7
    z_loc = (z + 6 + 4 * z_even) & 7
    p1 = (p1_re, p1_im)
    e1 = (e1_0, e1_1)

    def remote(src_ref, dst_ref, index, target):
        return pltpu.make_async_remote_copy(
            src_ref=src_ref, dst_ref=dst_ref, send_sem=ssem.at[index], recv_sem=rsem.at[index],
            device_id=target, device_id_type=MESH,
        )

    def arrived(ref, index):
        pltpu.make_async_copy(ref, ref, rsem.at[index]).wait()

    def left(ref, index):
        pltpu.make_async_copy(ref, ref, ssem.at[index]).wait()

    def near(d):
        flip = (d >> 2) & 1
        column = ((src >> 1) + d) & 3
        return 2 * column + ((src & 1) ^ flip), c ^ flip

    other_core = (src, z, 2 * c + 1 - e)
    other_chip = (src, z, 2 * (1 - c) + e)
    half = pl.ds(pl.multiple_of(256 * e, 256), 256)
    own_rows = [pl.ds(pl.multiple_of(32 * me + 16 * g, 16), 16) for g in range(2)]
    own_strip = pl.ds(pl.multiple_of(16 * u, 16), 16)

    loads = [
        pltpu.make_async_copy(one, two, lsem.at[index])
        for index, (one, two) in enumerate(
            (
                (part_hbm, part_ref),
                (sep_hbm, sep_ref),
                (gam_hbm, gam_ref),
                (tab_hbm, tab_ref),
                (e_ref, e_in),
                (p_ref.at[:, 0, :, half, :], p_in),
            )
        )
    ]
    for load in loads:
        load.start()

    barrier = pltpu.get_barrier_semaphore()

    def greet(target):
        pl.semaphore_signal(barrier, inc=1, device_id=target, device_id_type=MESH)

    def greet_blocks(d, carry):
        there, chip = near(d)
        greet((there, z_loc, 2 * chip + e))
        return carry

    def greet_plane(d, carry):
        i = (me + d) & 31
        greet((i >> 2, z, i & 3))
        return carry

    lax.fori_loop(0, 8, greet_blocks, 0)
    greet((src, z_rem, mom))
    for d in (1, 3, 4, 5, 7):
        greet((src, (z + d) & 7, mom))
    lax.fori_loop(1, 32, greet_plane, 0)

    for load in loads[:5]:
        load.wait()
    sep = sep_ref[k]
    odd = sep & 1
    is_a = ((z + (z >> 1) + (z >> 2)) & 1) == 1
    shift = jnp.where(is_a, sep >> 1, 16 - ((sep + 1) >> 1))
    par_loc = jnp.where(is_a, 0, (1 + odd) & 1)
    par_rem = jnp.where(is_a, odd, 1)
    time = (2 * u + jnp.where(is_a, 0, par_loc - sep)) & 31
    odd_own = sep_ref[z & 3] & 1
    snd_rem = jnp.where(z < NSEP, 1, odd_own)
    snd_loc = jnp.where(z < NSEP, 0, (1 + odd_own) & 1)
    partbuf[mom] = jnp.full((8, 128), part_ref[0], jnp.int32)
    for h in range(2):
        e_snd[h] = e_in[2 * h + par_rem]
    eloc[mom] = e_in[2 * c + par_loc]
    el_snd[...] = e_in[2 * (1 - c) + par_loc]
    loads[5].wait()
    for h in range(2):
        p_snd[:, h] = p_in[2 * h + snd_rem]
    for plane in range(2):
        pl_snd[:, pl.ds(512 * plane, 512)] = p_in[2 * c + snd_loc, plane]

    pl.semaphore_wait(barrier, 45)

    def send_partner(d, carry):
        remote(partbuf.at[mom], partbuf.at[mom], 0, (src, z, (mom + d) & 3)).start()
        return carry

    lax.fori_loop(1, 4, send_partner, 0)

    for g in range(2):

        def send_e1(d):
            i = (me + d) & 31
            rows = pl.ds(pl.multiple_of(32 * i + 16 * g, 16), 16)
            remote(e_snd.at[:, rows, :], e1[g].at[me], 1 + 18 * g, (i >> 2, z, i & 3)).start()

        def send_p1(d):
            there, chip = near(d)
            rows = pl.ds(pl.multiple_of(16 * (2 * there + chip), 16), 16)
            h = d >> 3
            remote(p_snd.at[g, h, rows, :], p1[g].at[2 * src + h], 2 + g, (there, z_rem, 2 * chip + e)).start()

        def send_both(d, carry):
            send_p1(d)
            send_e1(2 * d + 1)
            send_e1(2 * d + 2)
            return carry

        lax.fori_loop(0, 15, send_both, 0)
        send_p1(15)
        send_e1(31)
        e1[g][me] = e_snd[:, own_rows[g], :]

    own_e = remote(eloc.at[mom], eloc.at[mom], 4, other_core)
    own_e.start()
    cross_e = remote(el_snd, eloc.at[mom], 7, other_chip)
    cross_e.start()

    arrived(partbuf.at[pl.ds(0, 3)], 0)
    partners = [partbuf[o, 0, 0] for o in range(4)]

    def spread_p2(plane):
        arrived(p1[plane], 2 + plane)

        def send_p2(d, carry):
            j = (u + d) & 15
            p2s[plane, j] = p1[plane][(j + shift) & 15]
            remote(p2s.at[plane, j], pmine.at[plane, own_strip, :], 8 + plane, (j >> 1, z, 2 * (j & 1) + e)).start()
            return carry

        lax.fori_loop(1, 16, send_p2, 0)
        pmine[plane, own_strip, :] = p1[plane][(u + shift) & 15]

    def pick_e(g, i, a):
        block = ((i >> 1) + shift) & 15
        op = jnp.where(is_a, jnp.where((i & 1) == 0, partners[2 * a], partners[2 * a + 1]), (i & 1) + 2 * a)
        return e1[g][(block >> 1) * 4 + op, block & 1]

    def spread_e2(g):
        arrived(e1[g].at[pl.ds(0, 31)], 1 + 18 * g)

        def send_e2(d, carry):
            i = (me + d) & 31
            for a in range(2):
                e2s[g, i, a] = pick_e(g, i, a)
            remote(e2s.at[g, i], erem.at[:, own_rows[g], :], 5 + g, (i >> 2, z, i & 3)).start()
            return carry

        lax.fori_loop(1, 32, send_e2, 0)
        for a in range(2):
            erem[a, own_rows[g], :] = pick_e(g, me, a)

    spread_e2(0)
    spread_p2(0)
    spread_e2(1)
    spread_p2(1)

    chunks = [pl.ds(pl.multiple_of(256 * e + 128 * i, 128), 128) for i in range(2)]
    direct_p = []
    for i in range(2):
        part = pl_snd.at[pl.ds(128 * i, 128), :]
        direct_p.append(remote(part, ploc.at[chunks[i], :], 17 + i, (src, z_loc, mom)))
        direct_p[i].start()

    cross_e.wait_recv()
    from_chip = eloc.at[2 * (1 - c) + e]
    pass_e = remote(from_chip, from_chip, 10, other_core)
    pass_e.start()
    pass_p, pass_r = [], []

    def pass_local(i):
        direct_p[i].wait_recv()
        part = ploc.at[chunks[i], :]
        pass_p.append(remote(part, part, 11 + i, other_core))
        pass_p[i].start()

    own_e.wait_recv()
    pass_e.wait_recv()

    def loc_op(a):
        return jnp.where(is_a, e + 2 * a, partbuf[e + 2 * a, 0, 0])

    def turn(step, carry):
        rows = pl.ds(pl.multiple_of(128 * (step & 7), 128), 128)
        ptr[step] = eloc[loc_op(step >> 3), rows, :].astype(jnp.float32).T
        return carry

    lax.fori_loop(0, 16, turn, 0)

    def phased(op, s, take):
        sum_re = [jnp.zeros((128, 128), jnp.float32) for _ in range(4)]
        sum_im = [jnp.zeros((128, 128), jnp.float32) for _ in range(4)]
        for r in range(4):
            code = gam_ref[op, r]
            pattern = tab_ref[5 * code]
            power = tab_ref[5 * code + 1 + s]
            ca = jnp.where(power == 0, 1.0, jnp.where(power == 2, -1.0, 0.0))
            cb = jnp.where(power == 1, 1.0, jnp.where(power == 3, -1.0, 0.0))
            t_re, t_im = take(r)
            v_re = ca * t_re - cb * t_im
            v_im = ca * t_im + cb * t_re
            for s_left in range(4):
                here = jnp.where((s ^ pattern) == s_left, 1.0, 0.0)
                sum_re[s_left] += here * v_re
                sum_im[s_left] += here * v_im
        return sum_re, sum_im

    def build(step, carry):
        a, s = step >> 2, step & 3
        sum_re, sum_im = phased(loc_op(a), s, lambda r: (ptr[8 * a + 2 * r], ptr[8 * a + 2 * r + 1]))
        rows = pl.ds(pl.multiple_of(128 * s, 128), 128)
        more = pl.ds(pl.multiple_of(512 + 128 * s, 128), 128)
        for s_left in range(4):
            real, imag = sum_re[s_left].astype(jnp.bfloat16), sum_im[s_left].astype(jnp.bfloat16)
            elt[a, rows, pl.ds(128 * s_left, 128)] = real
            elt[a, rows, pl.ds(512 + 128 * s_left, 128)] = -imag
            elt[a, more, pl.ds(128 * s_left, 128)] = imag
            elt[a, more, pl.ds(512 + 128 * s_left, 128)] = real
        return carry

    lax.fori_loop(0, 8, build, 0)

    def pass_remote(plane):
        arrived(p1[plane].at[pl.ds(0, 15)], 8 + plane)
        pass_r.append(remote(pmine.at[plane], pother.at[plane], 13 + plane, other_core))
        pass_r[plane].start()

    pass_remote(0)

    for g in range(2):
        arrived(e1[g].at[pl.ds(0, 31)], 5 + g)

    def build_remote(step, carry):
        a, s = step >> 2, step & 3
        op = jnp.where(is_a, partbuf[e + 2 * a, 0, 0], e + 2 * a)

        def take(r):
            return (
                erem[a, pl.ds(256 * r, 128), :].astype(jnp.float32),
                erem[a, pl.ds(256 * r + 128, 128), :].astype(jnp.float32),
            )

        sum_re, sum_im = phased(op, s, take)
        first = pl.ds(pl.multiple_of(128 * s, 128), 128)
        second = pl.ds(pl.multiple_of(512 + 128 * s, 128), 128)
        for s_left in range(4):
            rows = pl.ds(128 * s_left, 128)
            real, imag = sum_re[s_left].astype(jnp.bfloat16), sum_im[s_left].astype(jnp.bfloat16)
            erd[a, 0, rows, first] = real
            erd[a, 0, rows, second] = imag
            erd[a, 1, rows, first] = -imag
            erd[a, 1, rows, second] = real
        return carry

    lax.fori_loop(0, 8, build_remote, 0)

    def times_elemental(block, which, plane):
        rows = pl.ds(pl.multiple_of(256 * which, 256), 256)

        def product(step, carry):
            cols = pl.ds(pl.multiple_of(256 * step, 256), 256)
            for a in range(2):
                part = jnp.dot(block[plane], erd[a, plane, :, cols], preferred_element_type=jnp.float32)
                if plane == 0:
                    bacc[a, rows, cols] = part
                else:
                    bacc[a, rows, cols] += part
            return carry

        lax.fori_loop(0, 4, product, 0)

    def close(i, totals):
        right = jnp.concatenate([ploc[pl.ds(128 * i, 128), :], ploc[pl.ds(256 + 128 * i, 128), :]], axis=0)
        new = []
        for a in range(2):
            g = lax.dot_general(elt[a], right, (((1,), (1,)), ((), ())), preferred_element_type=jnp.float32)
            acc_re, acc_im = totals[a]
            for part in range(2):
                g_re, g_im = g[:512, 128 * part : 128 * part + 128], g[512:, 128 * part : 128 * part + 128]
                b_re = bacc[a, :, pl.ds(256 * part + 128 * i, 128)]
                b_im = bacc[a, :, pl.ds(512 + 256 * part + 128 * i, 128)]
                acc_re += jnp.sum((b_re * g_re - b_im * g_im).reshape(64, 8, 128), axis=0)
                acc_im += jnp.sum((b_re * g_im + b_im * g_re).reshape(64, 8, 128), axis=0)
            new.append((acc_re, acc_im))
        return new

    times_elemental(pmine, e, 0)
    pass_r[0].wait_recv()
    times_elemental(pother, 1 - e, 0)
    pass_remote(1)
    times_elemental(pmine, e, 1)
    pass_local(0)
    pass_r[1].wait_recv()
    times_elemental(pother, 1 - e, 1)
    zero = jnp.zeros((8, 128), jnp.float32)
    totals = [(zero, zero), (zero, zero)]
    pass_p[0].wait_recv()
    pass_local(1)
    totals = close(0, totals)
    pass_p[1].wait_recv()
    totals = close(1, totals)
    lane = lax.broadcasted_iota(jnp.int32, (8, 128), 1)
    row = lax.broadcasted_iota(jnp.int32, (8, 128), 0)
    tile = jnp.zeros((8, 128), jnp.float32)
    for a in range(2):
        for part in range(2):
            here = (lane == time + 32 * a) & (row == 2 * k + part)
            tile += jnp.where(here, jnp.sum(totals[a][part]) / 512, 0.0)
    res[...] = tile

    def send_r1(d, carry):
        remote(res, r1.at[z], 15, (src, (z + d) & 7, mom)).start()
        return carry

    lax.fori_loop(1, 8, send_r1, 0)
    r1[z] = res[...]
    arrived(r1.at[pl.ds(0, 7)], 15)
    t2[...] = jnp.sum(r1[...], axis=0)

    def send_r2(d, carry):
        j = (u + d) & 15
        remote(t2, r2.at[u], 16, (j >> 1, z, 2 * (j & 1) + e)).start()
        return carry

    lax.fori_loop(1, 16, send_r2, 0)
    r2[u] = t2[...]
    arrived(r2.at[pl.ds(0, 15)], 16)
    total = jnp.sum(r2[...], axis=0)
    for kk in range(NSEP):
        two = total[2 * kk : 2 * kk + 2]
        out_ref[kk, 0] = jnp.where(c == 0, two[:, :32], two[:, 32:64])

    left(partbuf.at[pl.ds(0, 3)], 0)
    for g in range(2):
        left(e1[g].at[pl.ds(0, 31)], 1 + 18 * g)
        left(e1[g].at[pl.ds(0, 31)], 5 + g)
    for plane in range(2):
        left(p1[plane], 2 + plane)
        left(p1[plane].at[pl.ds(0, 15)], 8 + plane)
    for copy in [own_e, cross_e, pass_e] + direct_p + pass_p + pass_r:
        copy.wait_send()
    left(r1.at[pl.ds(0, 7)], 15)
    left(r2.at[pl.ds(0, 15)], 16)


def shards(peram_blocks, projections, gamma_index, partner, separations):
    bf, f32, i32 = jnp.bfloat16, jnp.float32, jnp.int32
    buffers = [
        ((4, 1024, 128), bf),
        ((4, 2, 256, 512), bf),
        ((2, 1024, 128), bf),
        ((2, 2, 256, 512), bf),
        ((256, 1024), bf),
        ((1024, 128), bf),
        ((32, 2, 16, 128), bf),
        ((32, 2, 16, 128), bf),
        ((16, 16, 512), bf),
        ((16, 16, 512), bf),
        ((2, 32, 2, 16, 128), bf),
        ((2, 16, 16, 512), bf),
        ((4, 1024, 128), bf),
        ((2, 1024, 128), bf),
        ((512, 1024), bf),
        ((2, 256, 512), bf),
        ((2, 256, 512), bf),
        ((2, 512, 1024), f32),
        ((16, 128, 128), f32),
        ((2, 1024, 1024), bf),
        ((2, 2, 512, 1024), bf),
        ((4, 8, 128), i32),
        ((8, 128), f32),
        ((8, 8, 128), f32),
        ((8, 128), f32),
        ((16, 8, 128), f32),
    ]
    out = pl.pallas_call(
        body,
        out_shape=jax.ShapeDtypeStruct((NSEP, 1, 2, 32), f32),
        in_specs=[pl.BlockSpec(memory_space=pltpu.HBM)] * 6,
        out_specs=pl.BlockSpec(memory_space=pltpu.VMEM),
        scratch_shapes=[pltpu.SMEM(shape, i32) for shape in ((4,), (4, 4), (1,), (80,))]
        + [pltpu.VMEM(shape, dtype) for shape, dtype in buffers]
        + [pltpu.SemaphoreType.DMA((count,)) for count in (6, 20, 20)],
        compiler_params=pltpu.CompilerParams(
            collective_id=0, has_side_effects=True, vmem_limit_bytes=64 * 1024 * 1024 - 65536
        ),
    )(
        separations,
        gamma_index,
        partner,
        jnp.asarray(gamma_table()),
        peram_blocks,
        projections.reshape(4, 1024, 128),
    )
    return jnp.transpose(out, (3, 0, 1, 2))


def solution(mesh):
    placed = (
        P("src", "snk", None, None, None),
        P("src", "mom", None, None, None, None),
        P(),
        P("mom"),
        P(),
    )
    return jax.shard_map(
        shards, mesh=mesh, in_specs=placed, out_specs=P(None, None, "mom", None), check_vma=False
    )
```

```python
import functools

import jax
import jax.numpy as jnp
import numpy as np
from jax import lax
from jax.experimental import pallas as pl
from jax.experimental.pallas import tpu as pltpu
from jax.sharding import PartitionSpec as P

MESH = pl.DeviceIdType.MESH
NSEP = 4


def gamma_table():
    unit = np.eye(4, dtype=complex)
    one = np.array([[0, 0, 0, 1j], [0, 0, 1j, 0], [0, -1j, 0, 0], [-1j, 0, 0, 0]])
    two = np.array([[0, 0, 0, -1], [0, 0, 1, 0], [0, 1, 0, 0], [-1, 0, 0, 0]], dtype=complex)
    three = np.array([[0, 0, 1j, 0], [0, 0, 0, -1j], [-1j, 0, 0, 0], [0, 1j, 0, 0]])
    four = np.array([[0, 0, 1, 0], [0, 0, 0, 1], [1, 0, 0, 0], [0, 1, 0, 0]], dtype=complex)
    rows = []
    for code in range(16):
        value = unit
        for position, factor in enumerate((one, two, three, four)):
            if code >> position & 1:
                value = value @ factor
        pattern = int(np.flatnonzero(np.abs(value[:, 0]))[0])
        powers = [(1, 1j, -1, -1j).index(complex(value[s ^ pattern, s])) for s in range(4)]
        rows.append([pattern] + powers)
    return np.array(rows, dtype=np.int32).reshape(-1)


def body(
    sep_hbm, gam_hbm, part_hbm, tab_hbm, p_ref, e_ref, out_ref,
    sep_ref, gam_ref, part_ref, tab_ref,
    e_in, p_in, e_snd, p_snd, pl_snd, el_snd, e1_0, e1_1, p1_re, p1_im, e2s, p2s, eloc, erem, ploc, pmine, pother,
    bacc, tabl, tabr, elt, erd, partbuf, res, r1, t2, r2, lsem, ssem, rsem,
):
    src, z, mom = lax.axis_index("src"), lax.axis_index("snk"), lax.axis_index("mom")
    c, e = mom >> 1, mom & 1
    u = 2 * src + c
    me = 4 * src + mom
    k = (z + 2) & 3
    z_even = 1 - (z & 1)
    z_rem = (z + 2 + 4 * z_even) & 7
    z_loc = (z + 6 + 4 * z_even) & 7
    p1 = (p1_re, p1_im)
    e1 = (e1_0, e1_1)

    def remote(src_ref, dst_ref, index, target):
        return pltpu.make_async_remote_copy(
            src_ref=src_ref, dst_ref=dst_ref, send_sem=ssem.at[index], recv_sem=rsem.at[index],
            device_id=target, device_id_type=MESH,
        )

    def arrived(ref, index):
        pltpu.make_async_copy(ref, ref, rsem.at[index]).wait()

    def left(ref, index):
        pltpu.make_async_copy(ref, ref, ssem.at[index]).wait()

    def near(d):
        flip = (d >> 2) & 1
        column = ((src >> 1) + d) & 3
        return 2 * column + ((src & 1) ^ flip), c ^ flip

    other_core = (src, z, 2 * c + 1 - e)
    other_chip = (src, z, 2 * (1 - c) + e)
    half = pl.ds(pl.multiple_of(256 * e, 256), 256)
    own_rows = [pl.ds(pl.multiple_of(32 * me + 16 * g, 16), 16) for g in range(2)]
    own_strip = pl.ds(pl.multiple_of(16 * u, 16), 16)

    loads = [
        pltpu.make_async_copy(one, two, lsem.at[index])
        for index, (one, two) in enumerate(
            (
                (part_hbm, part_ref),
                (sep_hbm, sep_ref),
                (gam_hbm, gam_ref),
                (tab_hbm, tab_ref),
                (e_ref, e_in),
                (p_ref.at[:, 0, :, half, :], p_in),
            )
        )
    ]
    for load in loads:
        load.start()

    barrier = pltpu.get_barrier_semaphore()

    def greet(target):
        pl.semaphore_signal(barrier, inc=1, device_id=target, device_id_type=MESH)

    def greet_blocks(d, carry):
        there, chip = near(d)
        greet((there, z_loc, 2 * chip + e))
        return carry

    def greet_plane(d, carry):
        i = (me + d) & 31
        greet((i >> 2, z, i & 3))
        return carry

    lax.fori_loop(0, 8, greet_blocks, 0)
    greet((src, z_rem, mom))
    for d in (1, 3, 4, 5, 7):
        greet((src, (z + d) & 7, mom))
    lax.fori_loop(1, 32, greet_plane, 0)

    for load in loads[:5]:
        load.wait()
    sep = sep_ref[k]
    odd = sep & 1
    is_a = ((z + (z >> 1) + (z >> 2)) & 1) == 1
    shift = jnp.where(is_a, sep >> 1, 16 - ((sep + 1) >> 1))
    par_loc = jnp.where(is_a, 0, (1 + odd) & 1)
    par_rem = jnp.where(is_a, odd, 1)
    time = (2 * u + jnp.where(is_a, 0, par_loc - sep)) & 31
    odd_own = sep_ref[z & 3] & 1
    snd_rem = jnp.where(z < NSEP, 1, odd_own)
    snd_loc = jnp.where(z < NSEP, 0, (1 + odd_own) & 1)
    partbuf[mom] = jnp.full((8, 128), part_ref[0], jnp.int32)
    for h in range(2):
        e_snd[h] = e_in[2 * h + par_rem]
    eloc[mom] = e_in[2 * c + par_loc]
    el_snd[...] = e_in[2 * (1 - c) + par_loc]
    loads[5].wait()
    for h in range(2):
        p_snd[:, h] = p_in[2 * h + snd_rem]
    for plane in range(2):
        pl_snd[:, pl.ds(512 * plane, 512)] = p_in[2 * c + snd_loc, plane]

    for a in range(2):
        for r in range(4):
            tabl[a, r, 4] = jnp.zeros((128, 128), jnp.float32)
            tabr[a, r, 4] = jnp.zeros((128, 128), jnp.float32)

    pl.semaphore_wait(barrier, 45)

    def send_partner(d, carry):
        remote(partbuf.at[mom], partbuf.at[mom], 0, (src, z, (mom + d) & 3)).start()
        return carry

    lax.fori_loop(1, 4, send_partner, 0)

    for g in range(2):

        def send_e1(d):
            i = (me + d) & 31
            rows = pl.ds(pl.multiple_of(32 * i + 16 * g, 16), 16)
            remote(e_snd.at[:, rows, :], e1[g].at[me], 1 + 18 * g, (i >> 2, z, i & 3)).start()

        def send_p1(d):
            there, chip = near(d)
            rows = pl.ds(pl.multiple_of(16 * (2 * there + chip), 16), 16)
            h = d >> 3
            remote(p_snd.at[g, h, rows, :], p1[g].at[2 * src + h], 2 + g, (there, z_rem, 2 * chip + e)).start()

        def send_both(d, carry):
            send_p1(d)
            send_e1(2 * d + 1)
            send_e1(2 * d + 2)
            return carry

        lax.fori_loop(0, 15, send_both, 0)
        send_p1(15)
        send_e1(31)
        e1[g][me] = e_snd[:, own_rows[g], :]

    own_e = remote(eloc.at[mom], eloc.at[mom], 4, other_core)
    own_e.start()
    cross_e = remote(el_snd, eloc.at[mom], 7, other_chip)
    cross_e.start()

    arrived(partbuf.at[pl.ds(0, 3)], 0)
    partners = [partbuf[o, 0, 0] for o in range(4)]

    def spread_p2(plane):
        arrived(p1[plane], 2 + plane)

        def send_p2(d, carry):
            j = (u + d) & 15
            p2s[plane, j] = p1[plane][(j + shift) & 15]
            remote(p2s.at[plane, j], pmine.at[plane, own_strip, :], 8 + plane, (j >> 1, z, 2 * (j & 1) + e)).start()
            return carry

        lax.fori_loop(1, 16, send_p2, 0)
        pmine[plane, own_strip, :] = p1[plane][(u + shift) & 15]

    def pick_e(g, i, a):
        block = ((i >> 1) + shift) & 15
        op = jnp.where(is_a, jnp.where((i & 1) == 0, partners[2 * a], partners[2 * a + 1]), (i & 1) + 2 * a)
        return e1[g][(block >> 1) * 4 + op, block & 1]

    def spread_e2(g):
        arrived(e1[g].at[pl.ds(0, 31)], 1 + 18 * g)

        def send_e2(d, carry):
            i = (me + d) & 31
            for a in range(2):
                e2s[g, i, a] = pick_e(g, i, a)
            remote(e2s.at[g, i], erem.at[:, own_rows[g], :], 5 + g, (i >> 2, z, i & 3)).start()
            return carry

        lax.fori_loop(1, 32, send_e2, 0)
        for a in range(2):
            erem[a, own_rows[g], :] = pick_e(g, me, a)

    spread_e2(0)
    spread_p2(0)
    spread_e2(1)
    spread_p2(1)

    chunks = [pl.ds(pl.multiple_of(256 * e + 128 * i, 128), 128) for i in range(2)]
    direct_p = []
    for i in range(2):
        part = pl_snd.at[pl.ds(128 * i, 128), :]
        direct_p.append(remote(part, ploc.at[chunks[i], :], 17 + i, (src, z_loc, mom)))
        direct_p[i].start()

    cross_e.wait_recv()
    from_chip = eloc.at[2 * (1 - c) + e]
    pass_e = remote(from_chip, from_chip, 10, other_core)
    pass_e.start()
    pass_p, pass_r = [], []

    def pass_local(i):
        direct_p[i].wait_recv()
        part = ploc.at[chunks[i], :]
        pass_p.append(remote(part, part, 11 + i, other_core))
        pass_p[i].start()

    own_e.wait_recv()
    pass_e.wait_recv()

    def loc_op(a):
        return jnp.where(is_a, e + 2 * a, partbuf[e + 2 * a, 0, 0])

    def fill(table, step, value):
        a, r, plane = step >> 3, (step >> 1) & 3, step & 1
        table[a, r, plane] = value
        table[a, r, 2 + plane] = -value

    def turn(step, carry):
        rows = pl.ds(pl.multiple_of(128 * (step & 7), 128), 128)
        fill(tabl, step, eloc[loc_op(step >> 3), rows, :].astype(jnp.float32).T)
        return carry

    lax.fori_loop(0, 16, turn, 0)

    def phased(table, a, op, s, s_left):
        parts = [None, None]
        for r in range(4):
            code = gam_ref[op, r]
            power = tab_ref[5 * code + 1 + s]
            hit = (s ^ tab_ref[5 * code]) == s_left
            for part in range(2):
                term = table[a, r, jnp.where(hit, (4 + part - power) & 3, 4)]
                parts[part] = term if r == 0 else parts[part] + term
        return parts[0].astype(jnp.bfloat16), parts[1].astype(jnp.bfloat16)

    def build(step, carry):
        a, s = step >> 2, step & 3
        rows = pl.ds(pl.multiple_of(128 * s, 128), 128)
        more = pl.ds(pl.multiple_of(512 + 128 * s, 128), 128)
        for s_left in range(4):
            real, imag = phased(tabl, a, loc_op(a), s, s_left)
            elt[a, rows, pl.ds(128 * s_left, 128)] = real
            elt[a, rows, pl.ds(512 + 128 * s_left, 128)] = -imag
            elt[a, more, pl.ds(128 * s_left, 128)] = imag
            elt[a, more, pl.ds(512 + 128 * s_left, 128)] = real
        return carry

    lax.fori_loop(0, 8, build, 0)

    def pass_remote(plane):
        arrived(p1[plane].at[pl.ds(0, 15)], 8 + plane)
        pass_r.append(remote(pmine.at[plane], pother.at[plane], 13 + plane, other_core))
        pass_r[plane].start()

    pass_remote(0)

    for g in range(2):
        arrived(e1[g].at[pl.ds(0, 31)], 5 + g)

    def build_remote(step, carry):
        a, s = step >> 2, step & 3
        op = jnp.where(is_a, partbuf[e + 2 * a, 0, 0], e + 2 * a)

        first = pl.ds(pl.multiple_of(128 * s, 128), 128)
        second = pl.ds(pl.multiple_of(512 + 128 * s, 128), 128)
        for s_left in range(4):
            rows = pl.ds(128 * s_left, 128)
            real, imag = phased(tabr, a, op, s, s_left)
            erd[a, 0, rows, first] = real
            erd[a, 0, rows, second] = imag
            erd[a, 1, rows, first] = -imag
            erd[a, 1, rows, second] = real
        return carry

    def take(step, carry):
        rows = pl.ds(pl.multiple_of(128 * (step & 7), 128), 128)
        fill(tabr, step, erem[step >> 3, rows, :].astype(jnp.float32))
        return carry

    lax.fori_loop(0, 16, take, 0)
    lax.fori_loop(0, 8, build_remote, 0)

    def times_elemental(block, which, plane):
        rows = pl.ds(pl.multiple_of(256 * which, 256), 256)

        def product(step, carry):
            cols = pl.ds(pl.multiple_of(256 * step, 256), 256)
            for a in range(2):
                part = jnp.dot(block[plane], erd[a, plane, :, cols], preferred_element_type=jnp.float32)
                if plane == 0:
                    bacc[a, rows, cols] = part
                else:
                    bacc[a, rows, cols] += part
            return carry

        lax.fori_loop(0, 4, product, 0)

    def close(i, totals):
        right = jnp.concatenate([ploc[pl.ds(128 * i, 128), :], ploc[pl.ds(256 + 128 * i, 128), :]], axis=0)
        new = []
        for a in range(2):
            g = lax.dot_general(elt[a], right, (((1,), (1,)), ((), ())), preferred_element_type=jnp.float32)
            acc_re, acc_im = totals[a]
            for part in range(2):
                g_re, g_im = g[:512, 128 * part : 128 * part + 128], g[512:, 128 * part : 128 * part + 128]
                b_re = bacc[a, :, pl.ds(256 * part + 128 * i, 128)]
                b_im = bacc[a, :, pl.ds(512 + 256 * part + 128 * i, 128)]
                acc_re += jnp.sum((b_re * g_re - b_im * g_im).reshape(64, 8, 128), axis=0)
                acc_im += jnp.sum((b_re * g_im + b_im * g_re).reshape(64, 8, 128), axis=0)
            new.append((acc_re, acc_im))
        return new

    times_elemental(pmine, e, 0)
    pass_r[0].wait_recv()
    times_elemental(pother, 1 - e, 0)
    pass_remote(1)
    times_elemental(pmine, e, 1)
    pass_local(0)
    pass_r[1].wait_recv()
    times_elemental(pother, 1 - e, 1)
    zero = jnp.zeros((8, 128), jnp.float32)
    totals = [(zero, zero), (zero, zero)]
    pass_p[0].wait_recv()
    pass_local(1)
    totals = close(0, totals)
    pass_p[1].wait_recv()
    totals = close(1, totals)
    lane = lax.broadcasted_iota(jnp.int32, (8, 128), 1)
    row = lax.broadcasted_iota(jnp.int32, (8, 128), 0)
    tile = jnp.zeros((8, 128), jnp.float32)
    for a in range(2):
        for part in range(2):
            here = (lane == time + 32 * a) & (row == 2 * k + part)
            tile += jnp.where(here, jnp.sum(totals[a][part]) / 512, 0.0)
    res[...] = tile

    def send_r1(d, carry):
        remote(res, r1.at[z], 15, (src, (z + d) & 7, mom)).start()
        return carry

    lax.fori_loop(1, 8, send_r1, 0)
    r1[z] = res[...]
    arrived(r1.at[pl.ds(0, 7)], 15)
    t2[...] = jnp.sum(r1[...], axis=0)

    def send_r2(d, carry):
        j = (u + d) & 15
        remote(t2, r2.at[u], 16, (j >> 1, z, 2 * (j & 1) + e)).start()
        return carry

    lax.fori_loop(1, 16, send_r2, 0)
    r2[u] = t2[...]
    arrived(r2.at[pl.ds(0, 15)], 16)
    total = jnp.sum(r2[...], axis=0)
    for kk in range(NSEP):
        two = total[2 * kk : 2 * kk + 2]
        out_ref[kk, 0] = jnp.where(c == 0, two[:, :32], two[:, 32:64])

    left(partbuf.at[pl.ds(0, 3)], 0)
    for g in range(2):
        left(e1[g].at[pl.ds(0, 31)], 1 + 18 * g)
        left(e1[g].at[pl.ds(0, 31)], 5 + g)
    for plane in range(2):
        left(p1[plane], 2 + plane)
        left(p1[plane].at[pl.ds(0, 15)], 8 + plane)
    for copy in [own_e, cross_e, pass_e] + direct_p + pass_p + pass_r:
        copy.wait_send()
    left(r1.at[pl.ds(0, 7)], 15)
    left(r2.at[pl.ds(0, 15)], 16)


def shards(peram_blocks, projections, gamma_index, partner, separations):
    bf, f32, i32 = jnp.bfloat16, jnp.float32, jnp.int32
    buffers = [
        ((4, 1024, 128), bf),
        ((4, 2, 256, 512), bf),
        ((2, 1024, 128), bf),
        ((2, 2, 256, 512), bf),
        ((256, 1024), bf),
        ((1024, 128), bf),
        ((32, 2, 16, 128), bf),
        ((32, 2, 16, 128), bf),
        ((16, 16, 512), bf),
        ((16, 16, 512), bf),
        ((2, 32, 2, 16, 128), bf),
        ((2, 16, 16, 512), bf),
        ((4, 1024, 128), bf),
        ((2, 1024, 128), bf),
        ((512, 1024), bf),
        ((2, 256, 512), bf),
        ((2, 256, 512), bf),
        ((2, 512, 1024), f32),
        ((2, 4, 5, 128, 128), f32),
        ((2, 4, 5, 128, 128), f32),
        ((2, 1024, 1024), bf),
        ((2, 2, 512, 1024), bf),
        ((4, 8, 128), i32),
        ((8, 128), f32),
        ((8, 8, 128), f32),
        ((8, 128), f32),
        ((16, 8, 128), f32),
    ]
    out = pl.pallas_call(
        body,
        out_shape=jax.ShapeDtypeStruct((NSEP, 1, 2, 32), f32),
        in_specs=[pl.BlockSpec(memory_space=pltpu.HBM)] * 6,
        out_specs=pl.BlockSpec(memory_space=pltpu.VMEM),
        scratch_shapes=[pltpu.SMEM(shape, i32) for shape in ((4,), (4, 4), (1,), (80,))]
        + [pltpu.VMEM(shape, dtype) for shape, dtype in buffers]
        + [pltpu.SemaphoreType.DMA((count,)) for count in (6, 20, 20)],
        compiler_params=pltpu.CompilerParams(
            collective_id=0, has_side_effects=True, vmem_limit_bytes=64 * 1024 * 1024 - 65536
        ),
    )(
        separations,
        gamma_index,
        partner,
        jnp.asarray(gamma_table()),
        peram_blocks,
        projections.reshape(4, 1024, 128),
    )
    return jnp.transpose(out, (3, 0, 1, 2))


def solution(mesh):
    placed = (
        P("src", "snk", None, None, None),
        P("src", "mom", None, None, None, None),
        P(),
        P("mom"),
        P(),
    )
    return jax.shard_map(
        shards, mesh=mesh, in_specs=placed, out_specs=P(None, None, "mom", None), check_vma=False
    )
```

```python
import functools

import jax
import jax.numpy as jnp
import numpy as np
from jax import lax
from jax.experimental import pallas as pl
from jax.experimental.pallas import tpu as pltpu
from jax.sharding import PartitionSpec as P

MESH = pl.DeviceIdType.MESH
NSEP = 4


def gamma_table():
    unit = np.eye(4, dtype=complex)
    one = np.array([[0, 0, 0, 1j], [0, 0, 1j, 0], [0, -1j, 0, 0], [-1j, 0, 0, 0]])
    two = np.array([[0, 0, 0, -1], [0, 0, 1, 0], [0, 1, 0, 0], [-1, 0, 0, 0]], dtype=complex)
    three = np.array([[0, 0, 1j, 0], [0, 0, 0, -1j], [-1j, 0, 0, 0], [0, 1j, 0, 0]])
    four = np.array([[0, 0, 1, 0], [0, 0, 0, 1], [1, 0, 0, 0], [0, 1, 0, 0]], dtype=complex)
    rows = []
    for code in range(16):
        value = unit
        for position, factor in enumerate((one, two, three, four)):
            if code >> position & 1:
                value = value @ factor
        pattern = int(np.flatnonzero(np.abs(value[:, 0]))[0])
        powers = [(1, 1j, -1, -1j).index(complex(value[s ^ pattern, s])) for s in range(4)]
        rows.append([pattern] + powers)
    return np.array(rows, dtype=np.int32).reshape(-1)


def body(
    sep_hbm, gam_hbm, part_hbm, tab_hbm, p_ref, e_ref, out_ref,
    sep_ref, gam_ref, part_ref, tab_ref,
    e_in, p_in, e_snd, p_snd, pl_snd, el_snd, e1_0, e1_1, p1_re, p1_im, e2s, p2s, eloc, erem, ploc, prem,
    bacc, tabl, tabr, elt, erd, partbuf, res, r1, t2, r2, lsem, ssem, rsem,
):
    src, z, mom = lax.axis_index("src"), lax.axis_index("snk"), lax.axis_index("mom")
    c, e = mom >> 1, mom & 1
    u = 2 * src + c
    me = 4 * src + mom
    k = (z + 2) & 3
    z_even = 1 - (z & 1)
    z_rem = (z + 2 + 4 * z_even) & 7
    z_loc = (z + 6 + 4 * z_even) & 7
    p1 = (p1_re, p1_im)
    e1 = (e1_0, e1_1)

    def remote(src_ref, dst_ref, index, target):
        return pltpu.make_async_remote_copy(
            src_ref=src_ref, dst_ref=dst_ref, send_sem=ssem.at[index], recv_sem=rsem.at[index],
            device_id=target, device_id_type=MESH,
        )

    def arrived(ref, index):
        pltpu.make_async_copy(ref, ref, rsem.at[index]).wait()

    def left(ref, index):
        pltpu.make_async_copy(ref, ref, ssem.at[index]).wait()

    def near(d):
        flip = (d >> 2) & 1
        column = ((src >> 1) + d) & 3
        return 2 * column + ((src & 1) ^ flip), c ^ flip

    other_core = (src, z, 2 * c + 1 - e)
    other_chip = (src, z, 2 * (1 - c) + e)
    half = pl.ds(pl.multiple_of(256 * e, 256), 256)
    own_rows = [pl.ds(pl.multiple_of(32 * me + 16 * g, 16), 16) for g in range(2)]
    own_strip = pl.ds(pl.multiple_of(256 * e + 16 * u, 16), 16)

    loads = [
        pltpu.make_async_copy(one, two, lsem.at[index])
        for index, (one, two) in enumerate(
            (
                (part_hbm, part_ref),
                (sep_hbm, sep_ref),
                (gam_hbm, gam_ref),
                (tab_hbm, tab_ref),
                (e_ref, e_in),
                (p_ref.at[:, 0, :, half, :], p_in),
            )
        )
    ]
    barrier = pltpu.get_barrier_semaphore()

    def greet(target):
        pl.semaphore_signal(barrier, inc=1, device_id=target, device_id_type=MESH)

    def greet_blocks(d, carry):
        there, chip = near(d)
        greet((there, z_loc, 2 * chip + e))
        return carry

    def greet_plane(d, carry):
        i = (me + d) & 31
        greet((i >> 2, z, i & 3))
        return carry

    lax.fori_loop(0, 8, greet_blocks, 0)
    greet((src, z_rem, mom))
    for d in (1, 3, 4, 5, 7):
        greet((src, (z + d) & 7, mom))
    for load in loads:
        load.start()
    lax.fori_loop(1, 32, greet_plane, 0)

    for load in loads[:5]:
        load.wait()
    sep = sep_ref[k]
    odd = sep & 1
    is_a = ((z + (z >> 1) + (z >> 2)) & 1) == 1
    shift = jnp.where(is_a, sep >> 1, 16 - ((sep + 1) >> 1))
    par_loc = jnp.where(is_a, 0, (1 + odd) & 1)
    par_rem = jnp.where(is_a, odd, 1)
    time = (2 * u + jnp.where(is_a, 0, par_loc - sep)) & 31
    odd_own = sep_ref[z & 3] & 1
    snd_rem = jnp.where(z < NSEP, 1, odd_own)
    snd_loc = jnp.where(z < NSEP, 0, (1 + odd_own) & 1)
    partbuf[mom] = jnp.full((8, 128), part_ref[0], jnp.int32)
    for h in range(2):
        e_snd[h] = e_in[2 * h + par_rem]
    eloc[mom] = e_in[2 * c + par_loc]
    el_snd[...] = e_in[2 * (1 - c) + par_loc]
    loads[5].wait()
    for h in range(2):
        p_snd[:, h] = p_in[2 * h + snd_rem]
    for plane in range(2):
        pl_snd[:, pl.ds(512 * plane, 512)] = p_in[2 * c + snd_loc, plane]

    for a in range(2):
        for r in range(4):
            tabl[a, r, 4] = jnp.zeros((128, 128), jnp.float32)
            tabr[a, r, 4] = jnp.zeros((128, 128), jnp.float32)

    pl.semaphore_wait(barrier, 45)

    def send_partner(d, carry):
        remote(partbuf.at[mom], partbuf.at[mom], 0, (src, z, (mom + d) & 3)).start()
        return carry

    lax.fori_loop(1, 4, send_partner, 0)

    for g in range(2):

        def send_e1(d):
            i = (me + 13 * d) & 31
            rows = pl.ds(pl.multiple_of(32 * i + 16 * g, 16), 16)
            remote(e_snd.at[:, rows, :], e1[g].at[me], 1 + 18 * g, (i >> 2, z, i & 3)).start()

        def send_p1(d):
            there, chip = near(d)
            rows = pl.ds(pl.multiple_of(16 * (2 * there + chip), 16), 16)
            h = d >> 3
            remote(p_snd.at[g, h, rows, :], p1[g].at[2 * src + h], 2 + g, (there, z_rem, 2 * chip + e)).start()

        def send_both(d, carry):
            send_p1(d)
            send_e1(2 * d + 1)
            send_e1(2 * d + 2)
            return carry

        lax.fori_loop(0, 15, send_both, 0)
        send_p1(15)
        send_e1(31)
        e1[g][me] = e_snd[:, own_rows[g], :]

    own_e = remote(eloc.at[mom], eloc.at[mom], 4, other_core)
    own_e.start()
    cross_e = remote(el_snd, eloc.at[mom], 7, other_chip)
    cross_e.start()

    arrived(partbuf.at[pl.ds(0, 3)], 0)
    partners = [partbuf[o, 0, 0] for o in range(4)]

    def spread_p2(plane):
        arrived(p1[plane], 2 + plane)

        def send_p2(d, carry):
            j = (u + 5 * d) & 15
            p2s[plane, j] = p1[plane][(j + shift) & 15]
            remote(p2s.at[plane, j], prem.at[plane, own_strip, :], 8 + plane, (j >> 1, z, 2 * (j & 1) + e)).start()
            return carry

        lax.fori_loop(1, 16, send_p2, 0)
        prem[plane, own_strip, :] = p1[plane][(u + shift) & 15]

    def pick_e(g, i, a):
        block = ((i >> 1) + shift) & 15
        op = jnp.where(is_a, jnp.where((i & 1) == 0, partners[2 * a], partners[2 * a + 1]), (i & 1) + 2 * a)
        return e1[g][(block >> 1) * 4 + op, block & 1]

    def spread_e2(g):
        arrived(e1[g].at[pl.ds(0, 31)], 1 + 18 * g)

        def send_e2(d, carry):
            i = (me + 13 * d) & 31
            for a in range(2):
                e2s[g, i, a] = pick_e(g, i, a)
            remote(e2s.at[g, i], erem.at[:, own_rows[g], :], 5 + g, (i >> 2, z, i & 3)).start()
            return carry

        lax.fori_loop(1, 32, send_e2, 0)
        for a in range(2):
            erem[a, own_rows[g], :] = pick_e(g, me, a)

    spread_e2(0)
    spread_p2(0)
    spread_e2(1)
    spread_p2(1)

    chunks = [pl.ds(pl.multiple_of(256 * e + 128 * i, 128), 128) for i in range(2)]
    direct_p = []
    for i in range(2):
        part = pl_snd.at[pl.ds(128 * i, 128), :]
        direct_p.append(remote(part, ploc.at[chunks[i], :], 17 + i, (src, z_loc, mom)))
        direct_p[i].start()

    cross_e.wait_recv()
    from_chip = eloc.at[2 * (1 - c) + e]
    pass_e = remote(from_chip, from_chip, 10, other_core)
    pass_e.start()
    pass_p, pass_r = [], []

    def pass_local(i):
        direct_p[i].wait_recv()
        part = ploc.at[chunks[i], :]
        pass_p.append(remote(part, part, 11 + i, other_core))
        pass_p[i].start()

    own_e.wait_recv()
    pass_e.wait_recv()

    def loc_op(a):
        return jnp.where(is_a, e + 2 * a, partbuf[e + 2 * a, 0, 0])

    def fill(table, step, value):
        a, r, plane = step >> 3, (step >> 1) & 3, step & 1
        table[a, r, plane] = value
        table[a, r, 2 + plane] = -value

    def turn(step, carry):
        rows = pl.ds(pl.multiple_of(128 * (step & 7), 128), 128)
        fill(tabl, step, eloc[loc_op(step >> 3), rows, :].astype(jnp.float32).T)
        return carry

    lax.fori_loop(0, 16, turn, 0)

    def phased(table, a, op, s, s_left):
        parts = [None, None]
        for r in range(4):
            code = gam_ref[op, r]
            power = tab_ref[5 * code + 1 + s]
            hit = (s ^ tab_ref[5 * code]) == s_left
            for part in range(2):
                term = table[a, r, jnp.where(hit, (4 + part - power) & 3, 4)]
                parts[part] = term if r == 0 else parts[part] + term
        return parts[0].astype(jnp.bfloat16), parts[1].astype(jnp.bfloat16)

    def build(step, carry):
        a, s = step >> 2, step & 3
        rows = pl.ds(pl.multiple_of(128 * s, 128), 128)
        more = pl.ds(pl.multiple_of(512 + 128 * s, 128), 128)
        for s_left in range(4):
            real, imag = phased(tabl, a, loc_op(a), s, s_left)
            elt[a, rows, pl.ds(128 * s_left, 128)] = real
            elt[a, rows, pl.ds(512 + 128 * s_left, 128)] = -imag
            elt[a, more, pl.ds(128 * s_left, 128)] = imag
            elt[a, more, pl.ds(512 + 128 * s_left, 128)] = real
        return carry

    lax.fori_loop(0, 8, build, 0)

    def pass_remote(plane):
        arrived(p1[plane].at[pl.ds(0, 15)], 8 + plane)
        own_half = prem.at[plane, half, :]
        pass_r.append(remote(own_half, own_half, 13 + plane, other_core))
        pass_r[plane].start()

    pass_remote(0)

    for g in range(2):
        arrived(e1[g].at[pl.ds(0, 31)], 5 + g)

    def build_remote(step, carry):
        a, s = step >> 2, step & 3
        op = jnp.where(is_a, partbuf[e + 2 * a, 0, 0], e + 2 * a)

        first = pl.ds(pl.multiple_of(128 * s, 128), 128)
        second = pl.ds(pl.multiple_of(512 + 128 * s, 128), 128)
        for s_left in range(4):
            rows = pl.ds(128 * s_left, 128)
            real, imag = phased(tabr, a, op, s, s_left)
            erd[a, 0, rows, first] = real
            erd[a, 0, rows, second] = imag
            erd[a, 1, rows, first] = -imag
            erd[a, 1, rows, second] = real
        return carry

    def take(step, carry):
        rows = pl.ds(pl.multiple_of(128 * (step & 7), 128), 128)
        fill(tabr, step, erem[step >> 3, rows, :].astype(jnp.float32))
        return carry

    lax.fori_loop(0, 16, take, 0)
    lax.fori_loop(0, 8, build_remote, 0)

    def times_elemental(plane):
        for a in range(2):
            part = jnp.dot(prem[plane], erd[a, plane], preferred_element_type=jnp.float32)
            if plane == 0:
                bacc[a] = part
            else:
                bacc[a] += part

    def close(i, totals):
        right = jnp.concatenate([ploc[pl.ds(128 * i, 128), :], ploc[pl.ds(256 + 128 * i, 128), :]], axis=0)
        new = []
        for a in range(2):
            g = lax.dot_general(elt[a], right, (((1,), (1,)), ((), ())), preferred_element_type=jnp.float32)
            acc_re, acc_im = totals[a]
            for part in range(2):
                g_re, g_im = g[:512, 128 * part : 128 * part + 128], g[512:, 128 * part : 128 * part + 128]
                b_re = bacc[a, :, pl.ds(256 * part + 128 * i, 128)]
                b_im = bacc[a, :, pl.ds(512 + 256 * part + 128 * i, 128)]
                acc_re += jnp.sum((b_re * g_re - b_im * g_im).reshape(64, 8, 128), axis=0)
                acc_im += jnp.sum((b_re * g_im + b_im * g_re).reshape(64, 8, 128), axis=0)
            new.append((acc_re, acc_im))
        return new

    pass_r[0].wait_recv()
    times_elemental(0)
    pass_remote(1)
    pass_local(0)
    pass_r[1].wait_recv()
    times_elemental(1)
    zero = jnp.zeros((8, 128), jnp.float32)
    totals = [(zero, zero), (zero, zero)]
    pass_p[0].wait_recv()
    pass_local(1)
    totals = close(0, totals)
    pass_p[1].wait_recv()
    totals = close(1, totals)
    lane = lax.broadcasted_iota(jnp.int32, (8, 128), 1)
    row = lax.broadcasted_iota(jnp.int32, (8, 128), 0)
    tile = jnp.zeros((8, 128), jnp.float32)
    for a in range(2):
        for part in range(2):
            here = (lane == time + 32 * a) & (row == 2 * k + part)
            value = jnp.sum(jnp.sum(totals[a][part], axis=0, keepdims=True), axis=1, keepdims=True)
            tile += jnp.where(here, value * (1.0 / 512), 0.0)
    res[...] = tile

    def send_r1(d, carry):
        remote(res, r1.at[z], 15, (src, (z + d) & 7, mom)).start()
        return carry

    lax.fori_loop(1, 8, send_r1, 0)
    r1[z] = res[...]
    arrived(r1.at[pl.ds(0, 7)], 15)
    t2[...] = jnp.sum(r1[...], axis=0)

    def send_r2(d, carry):
        j = (u + d) & 15
        remote(t2, r2.at[u], 16, (j >> 1, z, 2 * (j & 1) + e)).start()
        return carry

    lax.fori_loop(1, 16, send_r2, 0)
    r2[u] = t2[...]
    arrived(r2.at[pl.ds(0, 15)], 16)
    total = jnp.sum(r2[...], axis=0)
    for kk in range(NSEP):
        two = total[2 * kk : 2 * kk + 2]
        out_ref[kk, 0] = jnp.where(c == 0, two[:, :32], two[:, 32:64])

    left(partbuf.at[pl.ds(0, 3)], 0)
    for g in range(2):
        left(e1[g].at[pl.ds(0, 31)], 1 + 18 * g)
        left(e1[g].at[pl.ds(0, 31)], 5 + g)
    for plane in range(2):
        left(p1[plane], 2 + plane)
        left(p1[plane].at[pl.ds(0, 15)], 8 + plane)
    for copy in [own_e, cross_e, pass_e] + direct_p + pass_p + pass_r:
        copy.wait_send()
    left(r1.at[pl.ds(0, 7)], 15)
    left(r2.at[pl.ds(0, 15)], 16)


def shards(peram_blocks, projections, gamma_index, partner, separations):
    bf, f32, i32 = jnp.bfloat16, jnp.float32, jnp.int32
    buffers = [
        ((4, 1024, 128), bf),
        ((4, 2, 256, 512), bf),
        ((2, 1024, 128), bf),
        ((2, 2, 256, 512), bf),
        ((256, 1024), bf),
        ((1024, 128), bf),
        ((32, 2, 16, 128), bf),
        ((32, 2, 16, 128), bf),
        ((16, 16, 512), bf),
        ((16, 16, 512), bf),
        ((2, 32, 2, 16, 128), bf),
        ((2, 16, 16, 512), bf),
        ((4, 1024, 128), bf),
        ((2, 1024, 128), bf),
        ((512, 1024), bf),
        ((2, 512, 512), bf),
        ((2, 512, 1024), f32),
        ((2, 4, 5, 128, 128), f32),
        ((2, 4, 5, 128, 128), f32),
        ((2, 1024, 1024), bf),
        ((2, 2, 512, 1024), bf),
        ((4, 8, 128), i32),
        ((8, 128), f32),
        ((8, 8, 128), f32),
        ((8, 128), f32),
        ((16, 8, 128), f32),
    ]
    out = pl.pallas_call(
        body,
        out_shape=jax.ShapeDtypeStruct((NSEP, 1, 2, 32), f32),
        in_specs=[pl.BlockSpec(memory_space=pltpu.HBM)] * 6,
        out_specs=pl.BlockSpec(memory_space=pltpu.VMEM),
        scratch_shapes=[pltpu.SMEM(shape, i32) for shape in ((4,), (4, 4), (1,), (80,))]
        + [pltpu.VMEM(shape, dtype) for shape, dtype in buffers]
        + [pltpu.SemaphoreType.DMA((count,)) for count in (6, 20, 20)],
        compiler_params=pltpu.CompilerParams(
            collective_id=0, has_side_effects=True, vmem_limit_bytes=64 * 1024 * 1024 - 65536
        ),
    )(
        separations,
        gamma_index,
        partner,
        jnp.asarray(gamma_table()),
        peram_blocks,
        projections.reshape(4, 1024, 128),
    )
    return jnp.transpose(out, (3, 0, 1, 2))


def solution(mesh):
    placed = (
        P("src", "snk", None, None, None),
        P("src", "mom", None, None, None, None),
        P(),
        P("mom"),
        P(),
    )
    return jax.shard_map(
        shards, mesh=mesh, in_specs=placed, out_specs=P(None, None, "mom", None), check_vma=False
    )
```

```python
import functools

import jax
import jax.numpy as jnp
import numpy as np
from jax import lax
from jax.experimental import pallas as pl
from jax.experimental.pallas import tpu as pltpu
from jax.sharding import PartitionSpec as P

MESH = pl.DeviceIdType.MESH
NSEP = 4


def gamma_table():
    unit = np.eye(4, dtype=complex)
    one = np.array([[0, 0, 0, 1j], [0, 0, 1j, 0], [0, -1j, 0, 0], [-1j, 0, 0, 0]])
    two = np.array([[0, 0, 0, -1], [0, 0, 1, 0], [0, 1, 0, 0], [-1, 0, 0, 0]], dtype=complex)
    three = np.array([[0, 0, 1j, 0], [0, 0, 0, -1j], [-1j, 0, 0, 0], [0, 1j, 0, 0]])
    four = np.array([[0, 0, 1, 0], [0, 0, 0, 1], [1, 0, 0, 0], [0, 1, 0, 0]], dtype=complex)
    rows = []
    for code in range(16):
        value = unit
        for position, factor in enumerate((one, two, three, four)):
            if code >> position & 1:
                value = value @ factor
        pattern = int(np.flatnonzero(np.abs(value[:, 0]))[0])
        powers = [(1, 1j, -1, -1j).index(complex(value[s ^ pattern, s])) for s in range(4)]
        rows.append([pattern] + powers)
    return np.array(rows, dtype=np.int32).reshape(-1)


def body(
    sep_hbm, gam_hbm, part_hbm, tab_hbm, p_ref, e_ref, out_ref,
    sep_ref, gam_ref, part_ref, tab_ref,
    e_in, p_in, e_snd, p_snd, pl_snd, el_snd, e1_0, e1_1, p1_re, p1_im, e2s, p2s, eloc, erem, ploc, prem,
    bacc, tabl, tabr, elt, erd, partbuf, res, r1, t2, r2, lsem, ssem, rsem,
):
    src, z, mom = lax.axis_index("src"), lax.axis_index("snk"), lax.axis_index("mom")
    c, e = mom >> 1, mom & 1
    u = 2 * src + c
    me = 4 * src + mom
    k = (z + 2) & 3
    z_even = 1 - (z & 1)
    z_rem = (z + 2 + 4 * z_even) & 7
    z_loc = (z + 6 + 4 * z_even) & 7
    p1 = (p1_re, p1_im)
    e1 = (e1_0, e1_1)

    def remote(src_ref, dst_ref, index, target):
        return pltpu.make_async_remote_copy(
            src_ref=src_ref, dst_ref=dst_ref, send_sem=ssem.at[index], recv_sem=rsem.at[index],
            device_id=target, device_id_type=MESH,
        )

    def arrived(ref, index):
        pltpu.make_async_copy(ref, ref, rsem.at[index]).wait()

    def left(ref, index):
        pltpu.make_async_copy(ref, ref, ssem.at[index]).wait()

    def near(d):
        flip = (d >> 2) & 1
        column = ((src >> 1) + d) & 3
        return 2 * column + ((src & 1) ^ flip), c ^ flip

    other_core = (src, z, 2 * c + 1 - e)
    other_chip = (src, z, 2 * (1 - c) + e)
    half = pl.ds(pl.multiple_of(256 * e, 256), 256)
    own_rows = [pl.ds(pl.multiple_of(32 * me + 16 * g, 16), 16) for g in range(2)]
    own_strip = pl.ds(pl.multiple_of(256 * e + 16 * u, 16), 16)

    loads = [
        pltpu.make_async_copy(one, two, lsem.at[index])
        for index, (one, two) in enumerate(
            (
                (part_hbm, part_ref),
                (sep_hbm, sep_ref),
                (gam_hbm, gam_ref),
                (tab_hbm, tab_ref),
                (e_ref, e_in),
                (p_ref.at[:, 0, :, half, :], p_in),
            )
        )
    ]
    barrier = pltpu.get_barrier_semaphore()

    def greet(target):
        pl.semaphore_signal(barrier, inc=1, device_id=target, device_id_type=MESH)

    def greet_blocks(d, carry):
        there, chip = near(d)
        greet((there, z_loc, 2 * chip + e))
        return carry

    def greet_plane(d, carry):
        i = (me + d) & 31
        greet((i >> 2, z, i & 3))
        return carry

    lax.fori_loop(0, 8, greet_blocks, 0)
    greet((src, z_rem, mom))
    for d in (1, 3, 4, 5, 7):
        greet((src, (z + d) & 7, mom))
    for load in loads:
        load.start()
    lax.fori_loop(1, 32, greet_plane, 0)

    for load in loads[:5]:
        load.wait()
    sep = sep_ref[k]
    odd = sep & 1
    is_a = ((z + (z >> 1) + (z >> 2)) & 1) == 1
    shift = jnp.where(is_a, sep >> 1, 16 - ((sep + 1) >> 1))
    par_loc = jnp.where(is_a, 0, (1 + odd) & 1)
    par_rem = jnp.where(is_a, odd, 1)
    time = (2 * u + jnp.where(is_a, 0, par_loc - sep)) & 31
    odd_own = sep_ref[z & 3] & 1
    snd_rem = jnp.where(z < NSEP, 1, odd_own)
    snd_loc = jnp.where(z < NSEP, 0, (1 + odd_own) & 1)
    partbuf[mom] = jnp.full((8, 128), part_ref[0], jnp.int32)
    for h in range(2):
        e_snd[h] = e_in[2 * h + par_rem]
    eloc[mom] = e_in[2 * c + par_loc]
    el_snd[...] = e_in[2 * (1 - c) + par_loc]
    loads[5].wait()
    for h in range(2):
        p_snd[:, h] = p_in[2 * h + snd_rem]
    for plane in range(2):
        pl_snd[:, pl.ds(512 * plane, 512)] = p_in[2 * c + snd_loc, plane]

    for a in range(2):
        for r in range(4):
            tabl[a, r, 4] = jnp.zeros((128, 128), jnp.float32)
            tabr[a, r, 4] = jnp.zeros((128, 128), jnp.float32)

    pl.semaphore_wait(barrier, 45)

    def send_partner(d, carry):
        remote(partbuf.at[mom], partbuf.at[mom], 0, (src, z, (mom + d) & 3)).start()
        return carry

    lax.fori_loop(1, 4, send_partner, 0)

    for g in range(2):

        def send_e1(d):
            i = (me + 13 * d) & 31
            rows = pl.ds(pl.multiple_of(32 * i + 16 * g, 16), 16)
            remote(e_snd.at[:, rows, :], e1[g].at[me], 1 + 18 * g, (i >> 2, z, i & 3)).start()

        def send_p1(d):
            there, chip = near(d)
            rows = pl.ds(pl.multiple_of(16 * (2 * there + chip), 16), 16)
            h = d >> 3
            remote(p_snd.at[g, h, rows, :], p1[g].at[2 * src + h], 2 + g, (there, z_rem, 2 * chip + e)).start()

        def send_both(d, carry):
            send_p1(d)
            send_e1(2 * d + 1)
            send_e1(2 * d + 2)
            return carry

        lax.fori_loop(0, 15, send_both, 0)
        send_p1(15)
        send_e1(31)
        e1[g][me] = e_snd[:, own_rows[g], :]

    own_e = remote(eloc.at[mom], eloc.at[mom], 4, other_core)
    own_e.start()
    cross_e = remote(el_snd, eloc.at[mom], 7, other_chip)
    cross_e.start()

    arrived(partbuf.at[pl.ds(0, 3)], 0)
    partners = [partbuf[o, 0, 0] for o in range(4)]

    def spread_p2(plane):
        arrived(p1[plane], 2 + plane)

        def send_p2(d, carry):
            j = (u + 5 * d) & 15
            p2s[plane, j] = p1[plane][(j + shift) & 15]
            remote(p2s.at[plane, j], prem.at[plane, own_strip, :], 8 + plane, (j >> 1, z, 2 * (j & 1) + e)).start()
            return carry

        lax.fori_loop(1, 16, send_p2, 0)
        prem[plane, own_strip, :] = p1[plane][(u + shift) & 15]

    def pick_e(g, i, a):
        block = ((i >> 1) + shift) & 15
        op = jnp.where(is_a, jnp.where((i & 1) == 0, partners[2 * a], partners[2 * a + 1]), (i & 1) + 2 * a)
        return e1[g][(block >> 1) * 4 + op, block & 1]

    def spread_e2(g):
        arrived(e1[g].at[pl.ds(0, 31)], 1 + 18 * g)

        def send_e2(d, carry):
            i = (me + 13 * d) & 31
            for a in range(2):
                e2s[g, i, a] = pick_e(g, i, a)
            remote(e2s.at[g, i], erem.at[:, own_rows[g], :], 5 + g, (i >> 2, z, i & 3)).start()
            return carry

        lax.fori_loop(1, 32, send_e2, 0)
        for a in range(2):
            erem[a, own_rows[g], :] = pick_e(g, me, a)

    spread_e2(0)
    spread_p2(0)
    spread_e2(1)
    spread_p2(1)

    spans = ((0, 128), (128, 64), (192, 64))
    chunks = [pl.ds(pl.multiple_of(256 * e + first, 64), count) for first, count in spans]
    direct_p = []
    for i, (first, count) in enumerate(spans):
        part = pl_snd.at[pl.ds(first, count), :]
        direct_p.append(remote(part, ploc.at[chunks[i], :], (17, 18, 20)[i], (src, z_loc, mom)))
        direct_p[i].start()

    cross_e.wait_recv()
    from_chip = eloc.at[2 * (1 - c) + e]
    pass_e = remote(from_chip, from_chip, 10, other_core)
    pass_e.start()
    pass_p, pass_r = [], []

    def pass_local(i):
        direct_p[i].wait_recv()
        part = ploc.at[chunks[i], :]
        pass_p.append(remote(part, part, (11, 12, 21)[i], other_core))
        pass_p[i].start()

    own_e.wait_recv()
    pass_e.wait_recv()

    def loc_op(a):
        return jnp.where(is_a, e + 2 * a, partbuf[e + 2 * a, 0, 0])

    def fill(table, step, value):
        a, r, plane = step >> 3, (step >> 1) & 3, step & 1
        table[a, r, plane] = value
        table[a, r, 2 + plane] = -value

    def turn(step, carry):
        rows = pl.ds(pl.multiple_of(128 * (step & 7), 128), 128)
        fill(tabl, step, eloc[loc_op(step >> 3), rows, :].astype(jnp.float32).T)
        return carry

    lax.fori_loop(0, 16, turn, 0)

    def phased(table, a, op, s, s_left):
        parts = [None, None]
        for r in range(4):
            code = gam_ref[op, r]
            power = tab_ref[5 * code + 1 + s]
            hit = (s ^ tab_ref[5 * code]) == s_left
            for part in range(2):
                term = table[a, r, jnp.where(hit, (4 + part - power) & 3, 4)]
                parts[part] = term if r == 0 else parts[part] + term
        return parts[0].astype(jnp.bfloat16), parts[1].astype(jnp.bfloat16)

    def build(step, carry):
        a, s = step >> 2, step & 3
        rows = pl.ds(pl.multiple_of(128 * s, 128), 128)
        more = pl.ds(pl.multiple_of(512 + 128 * s, 128), 128)
        for s_left in range(4):
            real, imag = phased(tabl, a, loc_op(a), s, s_left)
            elt[a, rows, pl.ds(128 * s_left, 128)] = real
            elt[a, rows, pl.ds(512 + 128 * s_left, 128)] = -imag
            elt[a, more, pl.ds(128 * s_left, 128)] = imag
            elt[a, more, pl.ds(512 + 128 * s_left, 128)] = real
        return carry

    lax.fori_loop(0, 8, build, 0)

    def pass_remote(plane):
        arrived(p1[plane].at[pl.ds(0, 15)], 8 + plane)
        own_half = prem.at[plane, half, :]
        pass_r.append(remote(own_half, own_half, 13 + plane, other_core))
        pass_r[plane].start()

    pass_remote(0)

    for g in range(2):
        arrived(e1[g].at[pl.ds(0, 31)], 5 + g)

    def build_remote(step, carry):
        a, s = step >> 2, step & 3
        op = jnp.where(is_a, partbuf[e + 2 * a, 0, 0], e + 2 * a)

        first = pl.ds(pl.multiple_of(128 * s, 128), 128)
        second = pl.ds(pl.multiple_of(512 + 128 * s, 128), 128)
        for s_left in range(4):
            rows = pl.ds(128 * s_left, 128)
            real, imag = phased(tabr, a, op, s, s_left)
            erd[a, 0, rows, first] = real
            erd[a, 0, rows, second] = imag
            erd[a, 1, rows, first] = -imag
            erd[a, 1, rows, second] = real
        return carry

    def take(step, carry):
        rows = pl.ds(pl.multiple_of(128 * (step & 7), 128), 128)
        fill(tabr, step, erem[step >> 3, rows, :].astype(jnp.float32))
        return carry

    lax.fori_loop(0, 16, take, 0)
    lax.fori_loop(0, 8, build_remote, 0)

    def times_elemental(plane):
        for a in range(2):
            part = jnp.dot(prem[plane], erd[a, plane], preferred_element_type=jnp.float32)
            if plane == 0:
                bacc[a] = part
            else:
                bacc[a] += part

    def close(i, totals):
        right = jnp.concatenate([ploc[pl.ds(128 * i, 128), :], ploc[pl.ds(256 + 128 * i, 128), :]], axis=0)
        new = []
        for a in range(2):
            g = lax.dot_general(elt[a], right, (((1,), (1,)), ((), ())), preferred_element_type=jnp.float32)
            acc_re, acc_im = totals[a]
            for part in range(2):
                g_re, g_im = g[:512, 128 * part : 128 * part + 128], g[512:, 128 * part : 128 * part + 128]
                b_re = bacc[a, :, pl.ds(256 * part + 128 * i, 128)]
                b_im = bacc[a, :, pl.ds(512 + 256 * part + 128 * i, 128)]
                acc_re += jnp.sum((b_re * g_re - b_im * g_im).reshape(64, 8, 128), axis=0)
                acc_im += jnp.sum((b_re * g_im + b_im * g_re).reshape(64, 8, 128), axis=0)
            new.append((acc_re, acc_im))
        return new

    pass_r[0].wait_recv()
    times_elemental(0)
    pass_remote(1)
    pass_local(0)
    pass_r[1].wait_recv()
    times_elemental(1)
    zero = jnp.zeros((8, 128), jnp.float32)
    totals = [(zero, zero), (zero, zero)]
    pass_p[0].wait_recv()
    pass_local(1)
    pass_local(2)
    totals = close(0, totals)
    pass_p[1].wait_recv()
    pass_p[2].wait_recv()
    totals = close(1, totals)
    lane = lax.broadcasted_iota(jnp.int32, (8, 128), 1)
    row = lax.broadcasted_iota(jnp.int32, (8, 128), 0)
    tile = jnp.zeros((8, 128), jnp.float32)
    for a in range(2):
        for part in range(2):
            here = (lane == time + 32 * a) & (row == 2 * k + part)
            value = jnp.sum(jnp.sum(totals[a][part], axis=0, keepdims=True), axis=1, keepdims=True)
            tile += jnp.where(here, value * (1.0 / 512), 0.0)
    res[...] = tile

    def send_r1(d, carry):
        remote(res, r1.at[z], 15, (src, (z + d) & 7, mom)).start()
        return carry

    lax.fori_loop(1, 8, send_r1, 0)
    r1[z] = res[...]
    arrived(r1.at[pl.ds(0, 7)], 15)
    t2[...] = jnp.sum(r1[...], axis=0)

    def send_r2(d, carry):
        j = (u + d) & 15
        remote(t2, r2.at[u], 16, (j >> 1, z, 2 * (j & 1) + e)).start()
        return carry

    lax.fori_loop(1, 16, send_r2, 0)
    r2[u] = t2[...]
    arrived(r2.at[pl.ds(0, 15)], 16)
    total = jnp.sum(r2[...], axis=0)
    for kk in range(NSEP):
        two = total[2 * kk : 2 * kk + 2]
        out_ref[kk, 0] = jnp.where(c == 0, two[:, :32], two[:, 32:64])

    left(partbuf.at[pl.ds(0, 3)], 0)
    for g in range(2):
        left(e1[g].at[pl.ds(0, 31)], 1 + 18 * g)
        left(e1[g].at[pl.ds(0, 31)], 5 + g)
    for plane in range(2):
        left(p1[plane], 2 + plane)
        left(p1[plane].at[pl.ds(0, 15)], 8 + plane)
    for copy in [own_e, cross_e, pass_e] + direct_p + pass_p + pass_r:
        copy.wait_send()
    left(r1.at[pl.ds(0, 7)], 15)
    left(r2.at[pl.ds(0, 15)], 16)


def shards(peram_blocks, projections, gamma_index, partner, separations):
    bf, f32, i32 = jnp.bfloat16, jnp.float32, jnp.int32
    buffers = [
        ((4, 1024, 128), bf),
        ((4, 2, 256, 512), bf),
        ((2, 1024, 128), bf),
        ((2, 2, 256, 512), bf),
        ((256, 1024), bf),
        ((1024, 128), bf),
        ((32, 2, 16, 128), bf),
        ((32, 2, 16, 128), bf),
        ((16, 16, 512), bf),
        ((16, 16, 512), bf),
        ((2, 32, 2, 16, 128), bf),
        ((2, 16, 16, 512), bf),
        ((4, 1024, 128), bf),
        ((2, 1024, 128), bf),
        ((512, 1024), bf),
        ((2, 512, 512), bf),
        ((2, 512, 1024), f32),
        ((2, 4, 5, 128, 128), f32),
        ((2, 4, 5, 128, 128), f32),
        ((2, 1024, 1024), bf),
        ((2, 2, 512, 1024), bf),
        ((4, 8, 128), i32),
        ((8, 128), f32),
        ((8, 8, 128), f32),
        ((8, 128), f32),
        ((16, 8, 128), f32),
    ]
    out = pl.pallas_call(
        body,
        out_shape=jax.ShapeDtypeStruct((NSEP, 1, 2, 32), f32),
        in_specs=[pl.BlockSpec(memory_space=pltpu.HBM)] * 6,
        out_specs=pl.BlockSpec(memory_space=pltpu.VMEM),
        scratch_shapes=[pltpu.SMEM(shape, i32) for shape in ((4,), (4, 4), (1,), (80,))]
        + [pltpu.VMEM(shape, dtype) for shape, dtype in buffers]
        + [pltpu.SemaphoreType.DMA((count,)) for count in (6, 22, 22)],
        compiler_params=pltpu.CompilerParams(
            collective_id=0, has_side_effects=True, vmem_limit_bytes=64 * 1024 * 1024 - 65536
        ),
    )(
        separations,
        gamma_index,
        partner,
        jnp.asarray(gamma_table()),
        peram_blocks,
        projections.reshape(4, 1024, 128),
    )
    return jnp.transpose(out, (3, 0, 1, 2))


def solution(mesh):
    placed = (
        P("src", "snk", None, None, None),
        P("src", "mom", None, None, None, None),
        P(),
        P("mom"),
        P(),
    )
    return jax.shard_map(
        shards, mesh=mesh, in_specs=placed, out_specs=P(None, None, "mom", None), check_vma=False
    )
```
